256 devices in a mesh: segment: 2 (over x_lo), frame: 8 (over z), row: 16 (over y, x_hi, core).
Axes of the slice: x: 4 (x_hi: 2, x_lo: 2; x = x_hi * 2 + x_lo), y: 4, z: 8, core: 2. Of those that a mesh axis runs over, the one named last changes fastest.
Arguments:
- stream: bfloat16 [2, 16, 32, 32, 2048], P('segment', 'frame', 'row'), may hold values from -45 to 45
- mixer_gain: float32 [2, 2048], P('segment'), may hold values from 0.1 to 1.9
- spectrum: bfloat16 [2, 2, 32, 32, 2048], P('segment', None, 'row'), may hold values from -6 to 6
- mlp_gain: float32 [2, 2048], P('segment'), may hold values from 0.1 to 1.9
- gate_weight: bfloat16 [2, 2048, 8192], P('segment', 'frame', 'row'), may hold values from -0.125 to 0.125
- up_weight: bfloat16 [2, 2048, 8192], P('segment', 'frame', 'row'), may hold values from -0.125 to 0.125
- down_weight: bfloat16 [2, 2048, 8192], P('segment', 'frame', 'row'), may hold values from -0.0625 to 0.0625
Outputs:
- result: bfloat16 [2, 16, 32, 32, 2048], P('segment', 'frame', 'row')
The draws below stay inside these ranges and needn't reach their ends.
All inputs are finite; a program needn't handle non-finite values.
Results may differ from the reference program's by a relative error of at most 0.013.
Values may be sent and summed in bfloat16 or wider, within the bound.
A program may use at most 128 MiB of HBM per device.

```python
import math
import jax
import jax.numpy as jnp
from jax import lax

D = 2048
FF = 8192
H = 32
W = 32
F = 16
N_SEGMENT = 2
N_ROW = 16


def draw_stream(key, part):
    key = jax.random.fold_in(key, 11)
    key_values, key_rows, key_cols = jax.random.split(key, 3)
    full_shape = (N_SEGMENT, F, H, W, D)
    row_scale = jnp.exp(jax.random.uniform(key_rows, (N_SEGMENT, F, H, W, 1), jnp.float32, math.log(0.3), math.log(3.0)))
    col_scale = jnp.exp(jax.random.uniform(key_cols, (N_SEGMENT, 1, 1, 1, D), jnp.float32, math.log(0.3), math.log(3.0)))
    values = jax.random.normal(key_values, full_shape, jnp.float32)
    values = jnp.clip(values, -5.0, 5.0)
    return (values * row_scale * col_scale).astype(jnp.bfloat16)


def block_levels(stream_key, dims, cuts, smallest, top_value):
    factor_of, own = 1.0, jax.random.fold_in(stream_key, 6)
    for dim, parts in cuts:
        heights = jnp.exp(jax.random.uniform(jax.random.fold_in(own, dim), (parts,), jnp.float32, smallest / len(cuts), top_value / len(cuts)))
        factor_of = factor_of * jnp.repeat(heights, dims[dim] // parts).reshape([-1 if axis == dim else 1 for axis in range(len(dims))])
    return factor_of


def noise(own_key, dims, deviation, reach, shards=(), kind=jnp.bfloat16):
    drawn = deviation * jax.random.normal(own_key, dims, jnp.float32)
    if shards:
        drawn = drawn * block_levels(own_key, dims, shards, -0.22, 0.18)
    return jnp.clip(drawn, -reach, reach).astype(kind)


def setup_inputs(seed: int = 0) -> dict:
    key_of = jax.random.split(jax.random.key(seed), 8)
    return {
        "stream": draw_stream(jax.random.fold_in(key_of[7], 71), 0),
        "mixer_gain": jnp.clip(1.0 + 0.18 * jax.random.normal(key_of[1], (N_SEGMENT, D), jnp.float32), 0.1, 1.9),
        "spectrum": noise(key_of[2], (N_SEGMENT, 2, W, H, D), 1.0, 6.0, ((0, 2), (2, 16))),
        "mlp_gain": jnp.clip(1.0 + 0.18 * jax.random.normal(key_of[3], (N_SEGMENT, D), jnp.float32), 0.1, 1.9),
        "gate_weight": noise(key_of[4], (N_SEGMENT, D, FF), D ** -0.5, 0.125, ((0, 2), (1, 8), (2, 16))),
        "up_weight": noise(key_of[5], (N_SEGMENT, D, FF), D ** -0.5, 0.125, ((0, 2), (1, 8), (2, 16))),
        "down_weight": noise(key_of[6], (N_SEGMENT, D, FF), FF ** -0.5, 0.0625, ((0, 2), (1, 8), (2, 16))),
    }


def rms_scale(values, norm_gain):
    widened = values.astype(jnp.float32)
    mean_square = lax.optimization_barrier(jnp.mean(widened * widened, axis=-1, keepdims=True))
    return widened * lax.rsqrt(mean_square + 1e-05) * norm_gain.astype(jnp.float32)

def cosine_sine(length):
    indices = jnp.arange(length, dtype=jnp.int32)
    products = indices[:, None] * indices[None, :] % length
    angles = products.astype(jnp.float32) * (2.0 * math.pi / length)
    return (jnp.cos(angles).astype(jnp.bfloat16), jnp.sin(angles).astype(jnp.bfloat16))

def dft_tables(height, width):
    cosine_cols, sine_cols = cosine_sine(width)
    cosine_rows, sine_rows = cosine_sine(height)
    forward_cols = jnp.stack((cosine_cols, -sine_cols), axis=1)
    forward_rows = jnp.stack((jnp.stack((cosine_rows, -sine_rows), axis=1), jnp.stack((sine_rows, cosine_rows), axis=1)), axis=1)
    inverse_rows = jnp.stack((jnp.stack((cosine_rows, sine_rows), axis=1), jnp.stack((-sine_rows, cosine_rows), axis=1)), axis=1).astype(jnp.float32)
    inverse_cols = jnp.stack((cosine_cols, -sine_cols), axis=0)
    return (forward_cols, forward_rows, inverse_rows, inverse_cols)

def mixer(block, norm_gain, filt):
    exact = lax.Precision.HIGHEST
    height, width = (block.shape[1], block.shape[2])
    forward_cols, forward_rows, inverse_rows, inverse_cols = dft_tables(height, width)
    normed = rms_scale(block, norm_gain).astype(jnp.bfloat16)
    col_spec = jnp.einsum('fhwd,wck->fhckd', normed.astype(jnp.float32), forward_cols.astype(jnp.float32), precision=exact).astype(jnp.bfloat16)
    full_spec = jnp.einsum('fhckd,hcem->fekmd', col_spec.astype(jnp.float32), forward_rows.astype(jnp.float32), precision=exact)
    filt_wide = filt.astype(jnp.float32)
    real_part = full_spec[:, 0] * filt_wide[0] - full_spec[:, 1] * filt_wide[1]
    imag_part = full_spec[:, 0] * filt_wide[1] + full_spec[:, 1] * filt_wide[0]
    filtered = jnp.stack((real_part, imag_part), axis=1)
    back = jnp.einsum('fckmd,mceh->fehkd', filtered, inverse_rows, precision=exact).astype(jnp.bfloat16)
    conv = jnp.einsum('fehkd,ekw->fhwd', back.astype(jnp.float32), inverse_cols.astype(jnp.float32), precision=exact) * (1.0 / (height * width))
    return (block.astype(jnp.float32) + normed.astype(jnp.float32) * conv).astype(jnp.bfloat16)

def feed_forward(received, norm_gain, gate_w, up_w, down_w):
    depth = received.shape[-1]
    tokens = rms_scale(received, norm_gain).astype(jnp.bfloat16).reshape(-1, depth)
    gate = jnp.dot(tokens, gate_w, preferred_element_type=jnp.float32)
    upward = jnp.dot(tokens, up_w, preferred_element_type=jnp.float32)
    hidden = (jax.nn.silu(gate) * upward).astype(jnp.bfloat16)
    group = hidden.shape[1] // N_ROW
    hidden_blocks = hidden.reshape(-1, N_ROW, group).transpose(1, 0, 2)
    down_blocks = down_w.reshape(depth, N_ROW, group).transpose(1, 0, 2)

    def add_block(running, operands):
        partial_value = jnp.dot(operands[0], operands[1].T, preferred_element_type=jnp.float32)
        rounded = lax.optimization_barrier(partial_value.astype(jnp.bfloat16))
        return (running + rounded.astype(jnp.float32), None)
    running, _ = lax.scan(add_block, jnp.zeros((tokens.shape[0], depth), jnp.float32), (hidden_blocks, down_blocks))
    summed = received.astype(jnp.float32).reshape(-1, depth) + running
    return summed.astype(jnp.bfloat16).reshape(received.shape)

def reference(stream, mixer_gain, spectrum, mlp_gain, gate_weight, up_weight, down_weight):
    mixed = [mixer(stream[section], mixer_gain[section], spectrum[section]) for section in range(N_SEGMENT)]
    results = [feed_forward(mixed[(section - 1) % N_SEGMENT], mlp_gain[section], gate_weight[section], up_weight[section], down_weight[section]) for section in range(N_SEGMENT)]
    return jnp.stack(results)
```

```python
import functools
import math

import jax
import jax.numpy as jnp
import numpy as np
from jax import lax
from jax.experimental import pallas as pl
from jax.experimental.pallas import tpu as pltpu
from jax.sharding import PartitionSpec as P

MESH = pl.DeviceIdType.MESH
BF16, F32 = jnp.bfloat16, jnp.float32

N_ROW, N_Y, N_Z = 16, 4, 8
FRAMES = 2
BLOCK = 64
TOKENS = N_ROW * BLOCK
LANES = 128
D, HID, WROWS = 2048, 512, 256
CHUNKS = 4
STEPS = FRAMES * CHUNKS
CCOLS = D // CHUNKS


def tables():
    n = 32
    index = np.arange(n)
    angle = (index[:, None] * index[None, :] % n) * (2.0 * math.pi / n)
    cos, sin = np.cos(angle), np.sin(angle)
    cos[np.abs(cos) < 1e-9] = 0.0
    sin[np.abs(sin) < 1e-9] = 0.0
    eye4, eye8 = np.eye(4), np.eye(8)
    fwd = np.stack((cos, -sin))
    col = np.einsum("cwk,hg->kchgw", fwd, eye8).reshape(512, 256)
    mix = np.empty((2, 2, n, n))
    mix[0, 0], mix[0, 1], mix[1, 0], mix[1, 1] = cos, -sin, sin, cos
    row = np.einsum("cejhm,kl->ekmjlch", mix.reshape(2, 2, 4, 8, n), eye4).reshape(256, 256)
    inv = np.empty((2, 2, n, n))
    inv[0, 0], inv[0, 1], inv[1, 0], inv[1, 1] = cos, sin, -sin, cos
    irow = np.einsum("cemah,kl->ahkeclm", inv.reshape(2, 2, n, 8, 4), eye4).reshape(256, 256)
    icol = np.einsum("eakw,hg->hwagke", fwd.reshape(2, 8, 4, n), eye4).reshape(128, 256)
    return tuple(jnp.asarray(t, BF16) for t in (col, row, irow, icol))


def kernel(
    stream, mixer_gain, spectrum, mlp_gain, gate_w, up_w, down_w,
    t_col, t_row, t_irow, t_icol,
    out,
    own_stream, rx_stream, rx_spec, aux_tx, aux_rx, rs_full, normed, col_buf, back_buf,
    full, wgu, wd, tok, hid,
    part, sib_tx, sib_rx,
    x1_tx, x1_rx, y2_tx, y2_rx, y3_tx, y3_rx, x4_tx, x4_rx, y5_tx, y5_rx,
    loc, a2a_s, a2a_r, zs, zr, ags, agr, rss, rsr,
):
    seg, z, me = lax.axis_index("segment"), lax.axis_index("frame"), lax.axis_index("row")
    core, xh, y = me % 2, (me // 2) % 2, me // 4
    row_of = lambda yy, xx, cc: (yy * 2 + xx) * 2 + cc
    ym, yp, y2 = (y + 3) % 4, (y + 1) % 4, (y + 2) % 4
    zm, zp = (z + 7) % 8, (z + 1) % 8
    to_yp, to_ym = (seg, z, row_of(yp, xh, core)), (seg, z, row_of(ym, xh, core))
    to_x, to_sib = (seg, z, row_of(y, 1 - xh, core)), (seg, z, row_of(y, xh, 1 - core))
    to_zp, to_zm = (seg, zp, me), (seg, zm, me)

    def remote(src, dst, ssem, rsem, to):
        return pltpu.make_async_remote_copy(
            src_ref=src, dst_ref=dst, send_sem=ssem, recv_sem=rsem, device_id=to, device_id_type=MESH
        )

    load_stream = pltpu.make_async_copy(stream, own_stream, loc.at[0])
    load_stream.start()
    my_rows = pl.ds(pl.multiple_of(z * WROWS, WROWS), WROWS)
    own_w = [
        pltpu.make_async_copy(gate_w, wgu.at[0, my_rows], loc.at[1]),
        pltpu.make_async_copy(up_w, wgu.at[1, my_rows], loc.at[2]),
        pltpu.make_async_copy(down_w, wd.at[z], loc.at[3]),
    ]
    for copy in own_w:
        copy.start()

    barrier = pltpu.get_barrier_semaphore()

    def greet(j, _):
        pl.semaphore_signal(barrier, inc=1, device_id=(1 - seg, z, j), device_id_type=MESH)
        return 0

    lax.fori_loop(0, N_ROW, greet, 0)
    for to in (to_yp, to_ym, to_x, to_sib, to_zp, to_zm):
        pl.semaphore_signal(barrier, inc=1, device_id=to, device_id_type=MESH)
    pl.semaphore_wait(barrier, N_ROW + 6)

    def slab(kind, j):
        cols = pl.ds(pl.multiple_of(j * LANES, LANES), LANES)
        src = (
            stream.at[:, :, cols] if kind == 0 else spectrum.at[:, :, cols] if kind == 1 else aux_tx.at[j]
        )
        dst = (rx_stream, rx_spec, aux_rx)[kind].at[me]
        return remote(src, dst, a2a_s.at[kind, j], a2a_r.at[kind, me], (1 - seg, z, j))

    def send_slabs(kind):
        def step(j, _):
            slab(kind, (me + j) % N_ROW).start()
            return 0

        lax.fori_loop(0, N_ROW, step, 0)

    def wait_slabs(kind):
        buf = (rx_stream, rx_spec, aux_rx)[kind]

        def step(j, _):
            remote(buf.at[j], buf.at[j], a2a_s.at[kind, j], a2a_r.at[kind, j], (1 - seg, z, j)).wait_recv()
            return 0

        lax.fori_loop(0, N_ROW, step, 0)

    def w_rows(k):
        return pl.ds(pl.multiple_of(((z + k + 8) % 8) * WROWS, WROWS), WROWS)

    half = (pl.ds(0, WROWS // 2), pl.ds(WROWS // 2, WROWS // 2))

    def ring(step, way, recv):
        sign = -1 if way == 0 else 1
        k = {0: 1, 1: 1, 2: 2, 3: 3, 4: 4, 5: 1, 6: 2, 7: 3, 8: 4}[step]
        k = sign * (k if recv else k - 1)
        if step < 2:
            dst = wgu.at[step, w_rows(k)]
            src = dst if recv else (gate_w, up_w)[step]
        elif step < 4:
            src = dst = wgu.at[:, w_rows(k)]
        elif step == 4:
            src = dst = wgu.at[way, w_rows(k)]
        elif step == 5:
            dst = wd.at[(z + k + 8) % 8]
            src = dst if recv else down_w
        elif step < 8:
            src = dst = wd.at[(z + k + 8) % 8]
        else:
            src = dst = wd.at[(z + k + 8) % 8, half[way]]
        return remote(src, dst, zs.at[way, step], zr.at[way, step], (to_zp, to_zm)[way])

    def ring_send(step):
        for way in (0, 1):
            ring(step, way, False).start()

    def ring_wait(step):
        for way in (0, 1):
            ring(step, way, True).wait_recv()

    send_slabs(0)
    ring_send(0)
    ring_send(1)
    send_slabs(1)

    load_stream.wait()
    rows = FRAMES * BLOCK
    wide = own_stream[...].reshape(rows, D).astype(F32)
    mean_square = jnp.mean(wide * wide, axis=-1, keepdims=True)
    scale = lax.rsqrt(mean_square + 1e-05)
    across = jnp.broadcast_to(scale, (rows, rows)).T
    for j in range(N_ROW):
        aux_tx[j, 0:8, :] = across[0:8, :]
        aux_tx[j, 8:16, :] = jnp.broadcast_to(mixer_gain[:, j * LANES : (j + 1) * LANES], (8, LANES))
    send_slabs(2)

    wait_slabs(0)
    wait_slabs(2)

    def spread(j, _):
        rs_full[j] = jnp.broadcast_to(aux_rx[j, 0:1, :], (rows, rows)).T
        return 0

    lax.fori_loop(0, N_ROW, spread, 0)

    def mixer(f):
        def scale_step(j, _):
            values = rx_stream[j, f].astype(F32)
            factor = rs_full[j, f * BLOCK : (f + 1) * BLOCK, :]
            normed[j] = (values * factor * aux_rx[j, 8:9, :]).astype(BF16)
            return 0

        lax.fori_loop(0, N_ROW, scale_step, 0)
        for j in range(4):
            block = normed[4 * j : 4 * j + 4].reshape(256, LANES)
            col_buf[j] = jnp.dot(t_col[...], block, preferred_element_type=F32).astype(BF16)
        if f == 0:
            wait_slabs(1)
        for kg in range(8):
            pencils = jnp.concatenate([col_buf[j, kg * 64 : (kg + 1) * 64, :] for j in range(4)], axis=0)
            spec = jnp.dot(t_row[...], pencils, preferred_element_type=F32)
            re, im = spec[:128], spec[128:]
            f_re = jnp.concatenate([rx_spec[2 * kg, 0], rx_spec[2 * kg + 1, 0]], axis=0).astype(F32)
            f_im = jnp.concatenate([rx_spec[2 * kg, 1], rx_spec[2 * kg + 1, 1]], axis=0).astype(F32)
            filtered = jnp.concatenate([re * f_re - im * f_im, re * f_im + im * f_re], axis=0)
            back = jnp.dot(t_irow[...], filtered.astype(BF16), preferred_element_type=F32)
            back_buf[kg] = back.astype(BF16)
        for hb in range(8):
            pencils = jnp.concatenate([back_buf[kg, hb * 32 : (hb + 1) * 32, :] for kg in range(8)], axis=0)
            conv = jnp.dot(t_icol[...], pencils, preferred_element_type=F32) * (1.0 / 1024.0)
            values = rx_stream[2 * hb : 2 * hb + 2, f].reshape(128, LANES).astype(F32)
            scaled = normed[2 * hb : 2 * hb + 2].reshape(128, LANES).astype(F32)
            mixed = (values + scaled * conv).astype(BF16)
            full[me, f, hb * BLOCK : (hb + 1) * BLOCK, :] = mixed[:BLOCK]
            full[me, f, 512 + hb * BLOCK : 512 + (hb + 1) * BLOCK, :] = mixed[BLOCK:]

    r = lambda yy, xx: row_of(yy, xx, core)
    xo = 1 - xh
    planes = (pl.ds(0, 512), pl.ds(512, 512))
    routes = [
        (me, None, to_yp, r(ym, xh)),
        (me, None, to_ym, r(yp, xh)),
        (me, None, to_x, r(y, xo)),
        (r(ym, xh), 0, to_yp, r(y2, xh)),
        (r(yp, xh), 1, to_ym, r(y2, xh)),
        (r(y, xo), None, to_yp, r(ym, xo)),
        (r(y, xo), None, to_ym, r(yp, xo)),
        (r(y2, xh), 0, to_x, r(y2, xo)),
        (r(y2, xh), 1, to_x, r(y2, xo)),
    ]
    handed = [
        (me, None), (r(ym, xh), None), (r(yp, xh), None), (r(y, xo), None), (r(y2, xh), 0), (r(y2, xh), 1),
        (r(ym, xo), None), (r(yp, xo), None), (r(y2, xo), 0), (r(y2, xo), 1),
    ]
    flip = lambda slot: slot + 1 - 2 * core
    for slot, plane in handed:
        routes.append((slot, plane, to_sib, flip(slot)))

    def gather(f, m, recv=False):
        sent, plane, to, got = routes[m]
        slot = got if recv else sent
        ref = full.at[slot, f] if plane is None else full.at[slot, f, planes[plane]]
        return remote(ref, ref, ags.at[f, m], agr.at[f, m], to)

    def g_send(f, *ms):
        for m in ms:
            gather(f, m).start()

    def g_wait(f, *ms):
        for m in ms:
            gather(f, m, True).wait_recv()

    def mlp(f, t):
        span = pl.ds(pl.multiple_of(t * 256, 256), 256)
        total = jnp.zeros((256, LANES), F32)
        for j in range(N_ROW):
            v = full[j, f, span, :].astype(F32)
            total = total + v * v
        scale = lax.rsqrt(jnp.sum(total, axis=-1, keepdims=True) * (1.0 / D) + 1e-05)
        for j in range(N_ROW):
            v = full[j, f, span, :].astype(F32)
            gain = mlp_gain[:, j * LANES : (j + 1) * LANES]
            tok[:, j * LANES : (j + 1) * LANES] = (v * scale * gain).astype(BF16)
        gate = jnp.dot(tok[...], wgu[0], preferred_element_type=F32)
        up = jnp.dot(tok[...], wgu[1], preferred_element_type=F32)
        hid[f, span, :] = (gate / (1.0 + jnp.exp(-gate)) * up).astype(BF16)

    mixer(0)
    g_send(0, 0, 1, 2, 9)
    ring_wait(0)
    ring_wait(1)
    for copy in own_w:
        copy.wait()
    ring_send(2)
    ring_send(5)
    mixer(1)
    g_send(1, 0, 1, 2, 9)
    g_wait(0, 0, 1)
    g_send(0, 3, 4, 10, 11)
    g_wait(0, 2)
    g_send(0, 5, 6, 12)
    ring_wait(2)
    ring_send(3)
    ring_wait(5)
    ring_send(6)
    g_wait(0, 3, 4)
    g_send(0, 7, 8, 13, 14)
    g_wait(1, 0, 1)
    g_send(1, 3, 4, 10, 11)
    g_wait(1, 2)
    g_send(1, 5, 6, 12)
    g_wait(0, 5, 6)
    g_send(0, 15, 16)
    ring_wait(3)
    ring_send(4)
    ring_wait(6)
    ring_send(7)
    g_wait(0, 7, 8)
    g_send(0, 17, 18)
    g_wait(1, 3, 4)
    g_send(1, 7, 8, 13, 14)
    g_wait(0, *range(9, 19))
    ring_wait(4)

    def tiles(f, lo, hi):
        def step(t, _):
            mlp(f, t)
            return 0

        lax.fori_loop(lo, hi, step, 0)

    tiles(0, 0, 2)
    g_wait(1, 5, 6)
    g_send(1, 15, 16)
    tiles(0, 2, 4)
    ring_wait(7)
    ring_send(8)
    g_wait(1, 7, 8)
    g_send(1, 17, 18)
    g_wait(1, *range(9, 19))

    q_same = lambda dy: ((y + dy + 4) % 4) * 2 + xh
    q_diff = lambda dy: ((y + dy + 4) % 4) * 2 + xo
    blk = lambda q: pl.ds(pl.multiple_of(q * BLOCK, BLOCK), BLOCK)
    low, high = pl.ds(0, BLOCK // 2), pl.ds(BLOCK // 2, BLOCK // 2)

    def reduce_copy(g, m):
        bufs = [
            (sib_tx.at[g], sib_rx.at[g], to_sib),
            (x1_tx.at[g], x1_rx.at[g], to_x),
            (y2_tx.at[g, 0], y2_rx.at[g, 0], to_yp),
            (y2_tx.at[g, 1], y2_rx.at[g, 1], to_ym),
            (y3_tx.at[g, 0], y3_rx.at[g, 0], to_yp),
            (y3_tx.at[g, 1], y3_rx.at[g, 1], to_ym),
            (x4_tx.at[g], x4_rx.at[g], to_x),
            (y5_tx.at[g, 0], y5_rx.at[g, 0], to_yp),
            (y5_tx.at[g, 1], y5_rx.at[g, 1], to_ym),
        ]
        src, dst, to = bufs[m]
        return remote(src, dst, rss.at[g, m], rsr.at[g, m], to)

    def columns(i):
        return (z - i + 8) % 8, (z + i + 1) % 8

    def stage0(g):
        f, i = g // CHUNKS, g % CHUNKS
        for n, zz in enumerate(columns(i)):
            cols = slice(n * 256, (n + 1) * 256)
            other = hid[f, pl.ds(pl.multiple_of((1 - core) * 512, 512), 512), :]
            sib_tx[g, :, cols] = lax.dot_general(
                other, wd[zz], (((1,), (1,)), ((), ())), preferred_element_type=F32
            ).astype(BF16)
        reduce_copy(g, 0).start()
        for n, zz in enumerate(columns(i)):
            cols = slice(n * 256, (n + 1) * 256)
            mine = hid[f, pl.ds(pl.multiple_of(core * 512, 512), 512), :]
            part[g, :, cols] = lax.dot_general(
                mine, wd[zz], (((1,), (1,)), ((), ())), preferred_element_type=F32
            )

    def stage1(g):
        reduce_copy(g, 0).wait_recv()
        take = lambda q: part[g, blk(q), :] + sib_rx[g, blk(q), :].astype(F32)
        x1_tx[g] = take(q_diff(2)).astype(BF16)
        reduce_copy(g, 1).start()
        y2_tx[g, 0] = take(q_diff(1)).astype(BF16)
        reduce_copy(g, 2).start()
        y2_tx[g, 1] = take(q_diff(-1)).astype(BF16)
        reduce_copy(g, 3).start()
        for q in (q_same(0), q_same(1), q_same(2), q_same(3), q_diff(0)):
            part[g, blk(q), :] = take(q)

    def stage2(g):
        reduce_copy(g, 1).wait_recv()
        total = part[g, blk(q_same(2)), :] + x1_rx[g].astype(F32)
        y3_tx[g, 0] = total[: BLOCK // 2].astype(BF16)
        y3_tx[g, 1] = total[BLOCK // 2 :].astype(BF16)
        reduce_copy(g, 4).start()
        reduce_copy(g, 5).start()
        reduce_copy(g, 2).wait_recv()
        reduce_copy(g, 3).wait_recv()
        total = part[g, blk(q_diff(0)), :] + y2_rx[g, 0].astype(F32) + y2_rx[g, 1].astype(F32)
        x4_tx[g] = total.astype(BF16)
        reduce_copy(g, 6).start()

    def stage3(g):
        reduce_copy(g, 4).wait_recv()
        total = part[g, blk(q_same(1)), :]
        first = total[: BLOCK // 2] + y3_rx[g, 0].astype(F32)
        y5_tx[g, 0] = jnp.concatenate([first, total[BLOCK // 2 :]], axis=0).astype(BF16)
        reduce_copy(g, 7).start()
        reduce_copy(g, 5).wait_recv()
        total = part[g, blk(q_same(3)), :]
        second = total[BLOCK // 2 :] + y3_rx[g, 1].astype(F32)
        y5_tx[g, 1] = jnp.concatenate([total[: BLOCK // 2], second], axis=0).astype(BF16)
        reduce_copy(g, 8).start()

    def stage4(g):
        f, i = g // CHUNKS, g % CHUNKS
        for m in (6, 7, 8):
            reduce_copy(g, m).wait_recv()
        total = part[g, blk(q_same(0)), :] + x4_rx[g].astype(F32)
        total = total + y5_rx[g, 0].astype(F32) + y5_rx[g, 1].astype(F32)
        mine = pl.ds(pl.multiple_of(core * 512 + q_same(0) * BLOCK, BLOCK), BLOCK)
        for n, zz in enumerate(columns(i)):
            got = jnp.concatenate([full[2 * zz, f, mine, :], full[2 * zz + 1, f, mine, :]], axis=1)
            cols = pl.ds(pl.multiple_of(zz * 256, 256), 256)
            out[f, :, cols] = (got.astype(F32) + total[:, n * 256 : (n + 1) * 256]).astype(BF16)

    def step(g, _):
        @pl.when(g == 3)
        def _():
            ring_wait(8)

        @pl.when(g < STEPS)
        def _():
            stage0(g)

        @pl.when((g >= 1) & (g < STEPS + 1))
        def _():
            stage1(g - 1)

        @pl.when((g >= 2) & (g < STEPS + 2))
        def _():
            stage2(g - 2)

        @pl.when((g >= 3) & (g < STEPS + 3))
        def _():
            stage3(g - 3)

        @pl.when(g >= 4)
        def _():
            stage4(g - 4)

        @pl.when(g < CHUNKS)
        def _():
            mlp(1, g)

        return 0

    lax.fori_loop(0, STEPS + 4, step, 0)

    def drain_slabs(j, _):
        for kind in range(3):
            slab(kind, j).wait_send()
        return 0

    lax.fori_loop(0, N_ROW, drain_slabs, 0)
    for way in (0, 1):
        for n in range(9):
            ring(n, way, False).wait_send()
    for f in range(FRAMES):
        for m in range(19):
            gather(f, m).wait_send()

    def drain_reduce(g, _):
        for m in range(9):
            reduce_copy(g, m).wait_send()
        return 0

    lax.fori_loop(0, STEPS, drain_reduce, 0)


def body(stream, mixer_gain, spectrum, mlp_gain, gate_weight, up_weight, down_weight):
    any_spec = pl.BlockSpec(memory_space=pl.ANY)
    vmem_spec = pl.BlockSpec(memory_space=pltpu.VMEM)
    dma = pltpu.SemaphoreType.DMA
    scratch = [
        pltpu.VMEM((FRAMES, BLOCK, D), BF16),
        pltpu.VMEM((N_ROW, FRAMES, BLOCK, LANES), BF16),
        pltpu.VMEM((N_ROW, 2, BLOCK, LANES), BF16),
        pltpu.VMEM((N_ROW, 16, LANES), F32),
        pltpu.VMEM((N_ROW, 16, LANES), F32),
        pltpu.VMEM((N_ROW, LANES, LANES), F32),
        pltpu.VMEM((N_ROW, BLOCK, LANES), BF16),
        pltpu.VMEM((4, 512, LANES), BF16),
        pltpu.VMEM((8, 256, LANES), BF16),
        pltpu.VMEM((N_ROW, FRAMES, TOKENS, LANES), BF16),
        pltpu.VMEM((2, D, HID), BF16),
        pltpu.VMEM((N_Z, WROWS, HID), BF16),
        pltpu.VMEM((256, D), BF16),
        pltpu.VMEM((FRAMES, TOKENS, HID), BF16),
        pltpu.VMEM((STEPS, 512, CCOLS), F32),
        pltpu.VMEM((STEPS, 512, CCOLS), BF16),
        pltpu.VMEM((STEPS, 512, CCOLS), BF16),
        pltpu.VMEM((STEPS, BLOCK, CCOLS), BF16),
        pltpu.VMEM((STEPS, BLOCK, CCOLS), BF16),
        pltpu.VMEM((STEPS, 2, BLOCK, CCOLS), BF16),
        pltpu.VMEM((STEPS, 2, BLOCK, CCOLS), BF16),
        pltpu.VMEM((STEPS, 2, BLOCK // 2, CCOLS), BF16),
        pltpu.VMEM((STEPS, 2, BLOCK // 2, CCOLS), BF16),
        pltpu.VMEM((STEPS, BLOCK, CCOLS), BF16),
        pltpu.VMEM((STEPS, BLOCK, CCOLS), BF16),
        pltpu.VMEM((STEPS, 2, BLOCK, CCOLS), BF16),
        pltpu.VMEM((STEPS, 2, BLOCK, CCOLS), BF16),
        dma((4,)),
        dma((3, N_ROW)),
        dma((3, N_ROW)),
        dma((2, 9)),
        dma((2, 9)),
        dma((FRAMES, 19)),
        dma((FRAMES, 19)),
        dma((STEPS, 9)),
        dma((STEPS, 9)),
    ]
    result = pl.pallas_call(
        kernel,
        out_shape=jax.ShapeDtypeStruct((FRAMES, BLOCK, D), BF16),
        in_specs=[any_spec, vmem_spec, any_spec, vmem_spec, any_spec, any_spec, any_spec] + [vmem_spec] * 4,
        out_specs=vmem_spec,
        scratch_shapes=scratch,
        compiler_params=pltpu.CompilerParams(
            collective_id=0, has_side_effects=True, vmem_limit_bytes=62 * 2**20
        ),
        cost_estimate=pl.CostEstimate(flops=14_000_000_000, bytes_accessed=6 * 2**20, transcendentals=2**20),
    )(
        stream.reshape(FRAMES, BLOCK, D),
        mixer_gain,
        spectrum.reshape(2, BLOCK, D),
        mlp_gain,
        gate_weight[0],
        up_weight[0],
        down_weight[0],
        *tables(),
    )
    return result.reshape(stream.shape)


def solution(mesh):
    return jax.shard_map(
        body,
        mesh=mesh,
        in_specs=(
            P("segment", "frame", "row", None, None),
            P("segment", None),
            P("segment", None, "row", None, None),
            P("segment", None),
            P("segment", "frame", "row"),
            P("segment", "frame", "row"),
            P("segment", "frame", "row"),
        ),
        out_specs=P("segment", "frame", "row", None, None),
        check_vma=False,
    )
```

```python
import functools
import math

import jax
import jax.numpy as jnp
import numpy as np
from jax import lax
from jax.experimental import pallas as pl
from jax.experimental.pallas import tpu as pltpu
from jax.sharding import PartitionSpec as P

MESH = pl.DeviceIdType.MESH
BF16, F32 = jnp.bfloat16, jnp.float32

N_ROW, N_Y, N_Z = 16, 4, 8
FRAMES = 2
BLOCK = 64
TOKENS = N_ROW * BLOCK
LANES = 128
D, HID, WROWS = 2048, 512, 256
OWN = 3
STEPS = FRAMES * N_Z
CCOLS = D // N_Z
LAGS = (1, 4, 7, 10)
LIVE = LAGS[-1] + 1


def tables():
    n = 32
    index = np.arange(n)
    angle = (index[:, None] * index[None, :] % n) * (2.0 * math.pi / n)
    cos, sin = np.cos(angle), np.sin(angle)
    cos[np.abs(cos) < 1e-9] = 0.0
    sin[np.abs(sin) < 1e-9] = 0.0
    eye4, eye8 = np.eye(4), np.eye(8)
    fwd = np.stack((cos, -sin))
    col = np.einsum("cwk,hg->kchgw", fwd, eye8).reshape(512, 256)
    mix = np.empty((2, 2, n, n))
    mix[0, 0], mix[0, 1], mix[1, 0], mix[1, 1] = cos, -sin, sin, cos
    row = np.einsum("cejhm,kl->ekmjlch", mix.reshape(2, 2, 4, 8, n), eye4).reshape(256, 256)
    inv = np.empty((2, 2, n, n))
    inv[0, 0], inv[0, 1], inv[1, 0], inv[1, 1] = cos, sin, -sin, cos
    irow = np.einsum("cemah,kl->ahkeclm", inv.reshape(2, 2, n, 8, 4), eye4).reshape(256, 256)
    icol = np.einsum("eakw,hg->hwagke", fwd.reshape(2, 8, 4, n), eye4).reshape(128, 256)
    return jnp.asarray(np.concatenate((col, row, irow, icol)), BF16)


def kernel(
    stream, mixer_gain, spectrum, mlp_gain, gate_w, up_w, down_w,
    tables_ref,
    out,
    table, own_stream, rx_stream, rx_spec, aux_tx, aux_rx, rs_full, normed, col_buf, spec_buf, back_buf,
    full, wgu, wd, tok, tok_last, acc, hid,
    part, sib_tx, sib_rx,
    x1_tx, x1_rx, y2_tx, y2_rx, y3_tx, y3_rx, x4_tx, x4_rx, y5_tx, y5_rx,
    loc, a2a_s, a2a_r, spec_s, spec_r, zs, zr, ags, agr, rss, rsr,
):
    seg, z, me = lax.axis_index("segment"), lax.axis_index("frame"), lax.axis_index("row")
    core, xh, y = me % 2, (me // 2) % 2, me // 4
    row_of = lambda yy, xx, cc: (yy * 2 + xx) * 2 + cc
    ym, yp, y2 = (y + 3) % 4, (y + 1) % 4, (y + 2) % 4
    zm, zp = (z + 7) % 8, (z + 1) % 8
    to_yp, to_ym = (seg, z, row_of(yp, xh, core)), (seg, z, row_of(ym, xh, core))
    to_x, to_sib = (seg, z, row_of(y, 1 - xh, core)), (seg, z, row_of(y, xh, 1 - core))
    to_zp, to_zm = (seg, zp, me), (seg, zm, me)

    def remote(src, dst, ssem, rsem, to):
        return pltpu.make_async_remote_copy(
            src_ref=src, dst_ref=dst, send_sem=ssem, recv_sem=rsem, device_id=to, device_id_type=MESH
        )

    load_stream = pltpu.make_async_copy(stream, own_stream, loc.at[0])
    load_stream.start()
    load_table = pltpu.make_async_copy(tables_ref, table, loc.at[4])
    load_table.start()
    own_w = [
        pltpu.make_async_copy(gate_w, wgu.at[0, OWN], loc.at[1]),
        pltpu.make_async_copy(up_w, wgu.at[1, OWN], loc.at[2]),
        pltpu.make_async_copy(down_w, wd.at[OWN], loc.at[3]),
    ]
    for copy in own_w:
        copy.start()

    t_col, t_row, t_irow, t_icol = (table.at[a:b] for a, b in ((0, 512), (512, 768), (768, 1024), (1024, 1152)))

    barrier = pltpu.get_barrier_semaphore()

    def greet(j, _):
        pl.semaphore_signal(barrier, inc=1, device_id=(1 - seg, z, j), device_id_type=MESH)
        return 0

    lax.fori_loop(0, N_ROW, greet, 0)
    for to in (to_yp, to_ym, to_x, to_sib, to_zp, to_zm):
        pl.semaphore_signal(barrier, inc=1, device_id=to, device_id_type=MESH)
    pl.semaphore_wait(barrier, N_ROW + 6)

    def landing(kind, j):
        if kind < 2:
            return rx_stream.at[j, kind]
        return aux_rx.at[j] if kind == 2 else rx_spec.at[j, z % 2]

    def slab(kind, j):
        cols = pl.ds(pl.multiple_of(j * LANES, LANES), LANES)
        if kind < 2:
            src = stream.at[kind, :, cols]
        else:
            src = aux_tx.at[j] if kind == 2 else spectrum.at[z % 2, :, cols]
        return remote(src, landing(kind, me), a2a_s.at[kind, j], a2a_r.at[kind, me], (1 - seg, z, j))

    def send_slabs(kind):
        def step(j, _):
            slab(kind, (me + j) % N_ROW).start()
            return 0

        lax.fori_loop(0, N_ROW, step, 0)

    def wait_slabs(kind):
        def step(j, _):
            ref = landing(kind, j)
            remote(ref, ref, a2a_s.at[kind, j], a2a_r.at[kind, j], (1 - seg, z, j)).wait_recv()
            return 0

        lax.fori_loop(0, N_ROW, step, 0)

    def other_part(m, recv=False):
        to, slots = ((to_zp, pl.ds(0, N_ROW // 2)), (to_zm, pl.ds(N_ROW // 2, N_ROW // 2)))[m]
        ref = rx_spec.at[slots, (z + 1) % 2 if recv else z % 2]
        return remote(ref, ref, spec_s.at[m], spec_r.at[m], to)

    half = (pl.ds(0, WROWS // 2), pl.ds(WROWS // 2, WROWS // 2))

    def ring(step, way):
        k = step // 2 + 1 if step < 6 else 4 if step == 6 else step - 6
        sign = -1 if way == 0 else 1
        was, now = OWN + sign * (k - 1), (OWN + sign * k) % N_Z
        if step < 7:
            n = step % 2 if step < 6 else way
            dst = wgu.at[n, now]
            src = wgu.at[n, was] if step > 1 else (gate_w, up_w)[n]
        elif step < 10:
            dst = wd.at[now]
            src = wd.at[was] if step > 7 else down_w
        else:
            src, dst = wd.at[was, half[way]], wd.at[now, half[way]]
        return remote(src, dst, zs.at[way, step], zr.at[way, step], (to_zp, to_zm)[way])

    def ring_send(step):
        for way in (0, 1):
            ring(step, way).start()

    def ring_wait(step):
        for way in (0, 1):
            ring(step, way).wait_recv()

    send_slabs(3)
    send_slabs(0)
    ring_send(0)

    load_stream.wait()
    rows = FRAMES * BLOCK
    wide = own_stream[...].reshape(rows, D).astype(F32)
    mean_square = jnp.mean(wide * wide, axis=-1, keepdims=True)
    scale = lax.rsqrt(mean_square + 1e-05)
    across = jnp.broadcast_to(scale, (rows, rows)).T
    for j in range(N_ROW):
        aux_tx[j, 0:4, :] = across[0:4, :]
        aux_tx[j, 4:8, :] = jnp.broadcast_to(mixer_gain[:, j * LANES : (j + 1) * LANES], (4, LANES))
    send_slabs(2)
    send_slabs(1)
    wait_slabs(3)
    for m in range(2):
        other_part(m).start()
    ring_send(1)

    wait_slabs(0)
    wait_slabs(2)

    def spread(j, _):
        rs_full[j] = jnp.broadcast_to(aux_rx[j, 0:1, :], (rows, rows)).T
        return 0

    lax.fori_loop(0, N_ROW, spread, 0)

    def mixer_columns(f):
        def scale_step(j, _):
            values = rx_stream[j, f].astype(F32)
            factor = rs_full[j, f * BLOCK : (f + 1) * BLOCK, :]
            normed[f, j] = (values * factor * aux_rx[j, 4:5, :]).astype(BF16)
            return 0

        lax.fori_loop(0, N_ROW, scale_step, 0)
        for j in range(4):
            block = normed[f, 4 * j : 4 * j + 4].reshape(256, LANES)
            col_buf[f, j] = jnp.dot(t_col[...], block, preferred_element_type=F32).astype(BF16)

    def mixer_rows(f):
        for kg in range(8):
            pencils = jnp.concatenate([col_buf[f, j, kg * 64 : (kg + 1) * 64, :] for j in range(4)], axis=0)
            spec_buf[f, kg] = jnp.dot(t_row[...], pencils, preferred_element_type=F32)

    def mixer_filter(f):
        for kg in range(8):
            re, im = spec_buf[f, kg, :128], spec_buf[f, kg, 128:]
            f_re = jnp.concatenate([rx_spec[2 * kg, 0], rx_spec[2 * kg + 1, 0]], axis=0).astype(F32)
            f_im = jnp.concatenate([rx_spec[2 * kg, 1], rx_spec[2 * kg + 1, 1]], axis=0).astype(F32)
            filtered = jnp.concatenate([re * f_re - im * f_im, re * f_im + im * f_re], axis=0)
            back = jnp.dot(t_irow[...], filtered.astype(BF16), preferred_element_type=F32)
            back_buf[kg] = back.astype(BF16)
        for hb in range(8):
            pencils = jnp.concatenate([back_buf[kg, hb * 32 : (hb + 1) * 32, :] for kg in range(8)], axis=0)
            conv = jnp.dot(t_icol[...], pencils, preferred_element_type=F32) * (1.0 / 1024.0)
            values = rx_stream[2 * hb : 2 * hb + 2, f].reshape(128, LANES).astype(F32)
            scaled = normed[f, 2 * hb : 2 * hb + 2].reshape(128, LANES).astype(F32)
            mixed = (values + scaled * conv).astype(BF16)
            full[me, f, hb * BLOCK : (hb + 1) * BLOCK, :] = mixed[:BLOCK]
            full[me, f, 512 + hb * BLOCK : 512 + (hb + 1) * BLOCK, :] = mixed[BLOCK:]

    r = lambda yy, xx: row_of(yy, xx, core)
    xo = 1 - xh
    planes = (pl.ds(0, 512), pl.ds(512, 512))
    routes = [
        (me, None, to_yp, r(ym, xh)),
        (me, None, to_ym, r(yp, xh)),
        (me, None, to_x, r(y, xo)),
        (r(ym, xh), 0, to_yp, r(y2, xh)),
        (r(yp, xh), 1, to_ym, r(y2, xh)),
        (r(y, xo), None, to_yp, r(ym, xo)),
        (r(y, xo), None, to_ym, r(yp, xo)),
        (r(y2, xh), 0, to_x, r(y2, xo)),
        (r(y2, xh), 1, to_x, r(y2, xo)),
    ]
    handed = [
        (me, None), (r(ym, xh), None), (r(yp, xh), None), (r(y, xo), None), (r(y2, xh), 0), (r(y2, xh), 1),
        (r(ym, xo), None), (r(yp, xo), None), (r(y2, xo), 0), (r(y2, xo), 1),
    ]
    flip = lambda slot: slot + 1 - 2 * core
    for slot, plane in handed:
        routes.append((slot, plane, to_sib, flip(slot)))

    def gather(f, m, recv=False):
        sent, plane, to, got = routes[m]
        slot = got if recv else sent
        ref = full.at[slot, f] if plane is None else full.at[slot, f, planes[plane]]
        return remote(ref, ref, ags.at[f, m], agr.at[f, m], to)

    def g_send(f, *ms):
        for m in ms:
            gather(f, m).start()

    def g_wait(f, *ms):
        for m in ms:
            gather(f, m, True).wait_recv()

    most = (N_Z - 1) * WROWS

    def mlp_most(f, t):
        span = pl.ds(pl.multiple_of(t * 256, 256), 256)
        total = jnp.zeros((256, LANES), F32)
        for j in range(N_ROW):
            v = full[j, f, span, :].astype(F32)
            total = total + v * v
        scale = lax.rsqrt(jnp.sum(total, axis=-1, keepdims=True) * (1.0 / D) + 1e-05)
        for slot in range(N_Z):
            zz = (z + slot + N_Z - OWN) % N_Z
            for n in range(2):
                v = full[2 * zz + n, f, span, :].astype(F32)
                gain = mlp_gain[:, pl.ds(pl.multiple_of((2 * zz + n) * LANES, LANES), LANES)]
                v = (v * scale * gain).astype(BF16)
                if slot < N_Z - 1:
                    tok[:, slot * 256 + n * LANES : slot * 256 + (n + 1) * LANES] = v
                else:
                    tok_last[f, span, n * LANES : (n + 1) * LANES] = v
        for n in range(2):
            weight = wgu[n, : N_Z - 1].reshape(most, HID)
            acc[n, f, span, :] = jnp.dot(tok[...], weight, preferred_element_type=F32)

    def mlp_rest(f, t):
        span = pl.ds(pl.multiple_of(t * 256, 256), 256)
        last = tok_last[f, span, :]
        gate = acc[0, f, span, :] + jnp.dot(last, wgu[0, N_Z - 1], preferred_element_type=F32)
        up = acc[1, f, span, :] + jnp.dot(last, wgu[1, N_Z - 1], preferred_element_type=F32)
        hid[f, span, :] = (gate / (1.0 + jnp.exp(-gate)) * up).astype(BF16)

    load_table.wait()
    mixer_columns(0)
    mixer_rows(0)
    for m in range(2):
        other_part(m, True).wait_recv()
    for copy in own_w:
        copy.wait()
    mixer_filter(0)
    g_send(0, 0, 1, 2, 9)
    ring_wait(0)
    ring_send(2)
    wait_slabs(1)
    mixer_columns(1)
    mixer_rows(1)
    mixer_filter(1)
    g_send(1, 0, 1, 2, 9)
    ring_wait(1)
    ring_send(3)
    g_wait(0, 0, 1)
    g_send(0, 3, 4, 10, 11)
    g_wait(0, 2)
    g_send(0, 5, 6, 12)
    ring_wait(2)
    ring_send(4)
    g_wait(1, 0, 1)
    g_send(1, 3, 4, 10, 11)
    g_wait(1, 2)
    g_send(1, 5, 6, 12)
    ring_wait(3)
    ring_send(5)
    g_wait(0, 3, 4)
    g_send(0, 7, 8, 13, 14)
    g_wait(0, 5, 6)
    g_send(0, 15, 16)
    ring_wait(4)
    ring_wait(5)
    ring_send(6)
    ring_send(7)
    g_wait(1, 3, 4)
    g_send(1, 7, 8, 13, 14)
    g_wait(0, 7, 8)
    g_send(0, 17, 18)
    g_wait(0, *range(9, 19))

    def tiles(part_of, f, lo, hi):
        def step(t, _):
            part_of(f, t)
            return 0

        lax.fori_loop(lo, hi, step, 0)

    tiles(mlp_most, 0, 0, 2)
    g_wait(1, 5, 6)
    g_send(1, 15, 16)
    tiles(mlp_most, 0, 2, 4)
    g_wait(1, 7, 8)
    g_send(1, 17, 18)
    ring_wait(6)
    tiles(mlp_rest, 0, 0, 4)
    ring_wait(7)
    ring_send(8)

    q_same = lambda dy: ((y + dy + 4) % 4) * 2 + xh
    q_diff = lambda dy: ((y + dy + 4) % 4) * 2 + xo
    blk = lambda q: pl.ds(pl.multiple_of(q * BLOCK, BLOCK), BLOCK)
    low, high = pl.ds(0, BLOCK // 2), pl.ds(BLOCK // 2, BLOCK // 2)

    def reduce_copy(g, m):
        bufs = [
            (sib_tx.at[g], sib_rx.at[g], to_sib),
            (x1_tx.at[g], x1_rx.at[g], to_x),
            (y2_tx.at[g, 0], y2_rx.at[g, 0], to_yp),
            (y2_tx.at[g, 1], y2_rx.at[g, 1], to_ym),
            (y3_tx.at[g, 0], y3_rx.at[g, 0], to_yp),
            (y3_tx.at[g, 1], y3_rx.at[g, 1], to_ym),
            (x4_tx.at[g], x4_rx.at[g], to_x),
            (y5_tx.at[g, 0], y5_rx.at[g, 0], to_yp),
            (y5_tx.at[g, 1], y5_rx.at[g, 1], to_ym),
        ]
        src, dst, to = bufs[m]
        return remote(src, dst, rss.at[g, m], rsr.at[g, m], to)

    def place(g):
        late = g - 6
        f = jnp.where(g < 6, g // 3, jnp.where(g < 14, late // 2 % 2, g - 14))
        n = jnp.where(g < 6, g % 3, jnp.where(g < 14, 3 + late // 4 * 2 + late % 2, 7))
        return f, (n + 1) // 2 * (n % 2 * 2 - 1)

    def stage0(g):
        f, off = place(g)
        weight = wd[OWN + off]
        dims = (((1,), (1,)), ((), ()))
        other = hid[f, pl.ds(pl.multiple_of((1 - core) * 512, 512), 512), :]
        sib_tx[g] = lax.dot_general(other, weight, dims, preferred_element_type=F32).astype(BF16)
        reduce_copy(g, 0).start()
        mine = hid[f, pl.ds(pl.multiple_of(core * 512, 512), 512), :]
        part[g % LIVE] = lax.dot_general(mine, weight, dims, preferred_element_type=F32)

    def stage1(g):
        reduce_copy(g, 0).wait_recv()
        take = lambda q: part[g % LIVE, blk(q), :] + sib_rx[g, blk(q), :].astype(F32)
        x1_tx[g] = take(q_diff(2)).astype(BF16)
        reduce_copy(g, 1).start()
        y2_tx[g, 0] = take(q_diff(1)).astype(BF16)
        reduce_copy(g, 2).start()
        y2_tx[g, 1] = take(q_diff(-1)).astype(BF16)
        reduce_copy(g, 3).start()
        for q in (q_same(0), q_same(1), q_same(2), q_same(3), q_diff(0)):
            part[g % LIVE, blk(q), :] = take(q)

    def stage2(g):
        reduce_copy(g, 1).wait_recv()
        total = part[g % LIVE, blk(q_same(2)), :] + x1_rx[g].astype(F32)
        y3_tx[g, 0] = total[: BLOCK // 2].astype(BF16)
        y3_tx[g, 1] = total[BLOCK // 2 :].astype(BF16)
        reduce_copy(g, 4).start()
        reduce_copy(g, 5).start()
        reduce_copy(g, 2).wait_recv()
        reduce_copy(g, 3).wait_recv()
        total = part[g % LIVE, blk(q_diff(0)), :] + y2_rx[g, 0].astype(F32) + y2_rx[g, 1].astype(F32)
        x4_tx[g] = total.astype(BF16)
        reduce_copy(g, 6).start()

    def stage3(g):
        reduce_copy(g, 4).wait_recv()
        total = part[g % LIVE, blk(q_same(1)), :]
        first = total[: BLOCK // 2] + y3_rx[g, 0].astype(F32)
        y5_tx[g, 0] = jnp.concatenate([first, total[BLOCK // 2 :]], axis=0).astype(BF16)
        reduce_copy(g, 7).start()
        reduce_copy(g, 5).wait_recv()
        total = part[g % LIVE, blk(q_same(3)), :]
        second = total[BLOCK // 2 :] + y3_rx[g, 1].astype(F32)
        y5_tx[g, 1] = jnp.concatenate([total[: BLOCK // 2], second], axis=0).astype(BF16)
        reduce_copy(g, 8).start()

    def stage4(g):
        f, off = place(g)
        zz = (z + off + N_Z) % N_Z
        for m in (6, 7, 8):
            reduce_copy(g, m).wait_recv()
        total = part[g % LIVE, blk(q_same(0)), :] + x4_rx[g].astype(F32)
        total = total + y5_rx[g, 0].astype(F32) + y5_rx[g, 1].astype(F32)
        mine = pl.ds(pl.multiple_of(core * 512 + q_same(0) * BLOCK, BLOCK), BLOCK)
        got = jnp.concatenate([full[2 * zz, f, mine, :], full[2 * zz + 1, f, mine, :]], axis=1)
        cols = pl.ds(pl.multiple_of(zz * 256, 256), 256)
        out[f, :, cols] = (got.astype(F32) + total).astype(BF16)

    def step(g, _):
        for n, when in enumerate((4, 9)):

            @pl.when(g == when)
            def _(n=n):
                ring_wait(8 + n)
                ring_send(9 + n)

        @pl.when(g == 14)
        def _():
            ring_wait(10)

        @pl.when(g < STEPS)
        def _():
            stage0(g)

        for lag, stage in zip(LAGS, (stage1, stage2, stage3, stage4)):

            @pl.when((g >= lag) & (g < STEPS + lag))
            def _(lag=lag, stage=stage):
                stage(g - lag)

        @pl.when(g == 0)
        def _():
            g_wait(1, *range(9, 19))
            tiles(mlp_most, 1, 0, 2)

        @pl.when(g == 1)
        def _():
            tiles(mlp_most, 1, 2, 3)

        @pl.when(g == 2)
        def _():
            tiles(mlp_most, 1, 3, 4)
            tiles(mlp_rest, 1, 0, 4)

        return 0

    lax.fori_loop(0, STEPS + LAGS[-1], step, 0)

    def drain_slabs(j, _):
        for kind in range(4):
            slab(kind, j).wait_send()
        return 0

    lax.fori_loop(0, N_ROW, drain_slabs, 0)
    for m in range(2):
        other_part(m).wait_send()
    for way in (0, 1):
        for n in range(11):
            ring(n, way).wait_send()
    for f in range(FRAMES):
        for m in range(19):
            gather(f, m).wait_send()

    def drain_reduce(g, _):
        for m in range(9):
            reduce_copy(g, m).wait_send()
        return 0

    lax.fori_loop(0, STEPS, drain_reduce, 0)


def body(stream, mixer_gain, spectrum, mlp_gain, gate_weight, up_weight, down_weight):
    any_spec = pl.BlockSpec(memory_space=pl.ANY)
    vmem_spec = pl.BlockSpec(memory_space=pltpu.VMEM)
    dma = pltpu.SemaphoreType.DMA
    scratch = [
        pltpu.VMEM((1152, 256), BF16),
        pltpu.VMEM((FRAMES, BLOCK, D), BF16),
        pltpu.VMEM((N_ROW, FRAMES, BLOCK, LANES), BF16),
        pltpu.VMEM((N_ROW, 2, BLOCK, LANES), BF16),
        pltpu.VMEM((N_ROW, 8, LANES), F32),
        pltpu.VMEM((N_ROW, 8, LANES), F32),
        pltpu.VMEM((N_ROW, LANES, LANES), F32),
        pltpu.VMEM((FRAMES, N_ROW, BLOCK, LANES), BF16),
        pltpu.VMEM((FRAMES, 4, 512, LANES), BF16),
        pltpu.VMEM((FRAMES, 8, 256, LANES), F32),
        pltpu.VMEM((8, 256, LANES), BF16),
        pltpu.VMEM((N_ROW, FRAMES, TOKENS, LANES), BF16),
        pltpu.VMEM((2, N_Z, WROWS, HID), BF16),
        pltpu.VMEM((N_Z, WROWS, HID), BF16),
        pltpu.VMEM((256, D - WROWS), BF16),
        pltpu.VMEM((FRAMES, TOKENS, WROWS), BF16),
        pltpu.VMEM((2, FRAMES, TOKENS, HID), F32),
        pltpu.VMEM((FRAMES, TOKENS, HID), BF16),
        pltpu.VMEM((LIVE, 512, CCOLS), F32),
        pltpu.VMEM((STEPS, 512, CCOLS), BF16),
        pltpu.VMEM((STEPS, 512, CCOLS), BF16),
        pltpu.VMEM((STEPS, BLOCK, CCOLS), BF16),
        pltpu.VMEM((STEPS, BLOCK, CCOLS), BF16),
        pltpu.VMEM((STEPS, 2, BLOCK, CCOLS), BF16),
        pltpu.VMEM((STEPS, 2, BLOCK, CCOLS), BF16),
        pltpu.VMEM((STEPS, 2, BLOCK // 2, CCOLS), BF16),
        pltpu.VMEM((STEPS, 2, BLOCK // 2, CCOLS), BF16),
        pltpu.VMEM((STEPS, BLOCK, CCOLS), BF16),
        pltpu.VMEM((STEPS, BLOCK, CCOLS), BF16),
        pltpu.VMEM((STEPS, 2, BLOCK, CCOLS), BF16),
        pltpu.VMEM((STEPS, 2, BLOCK, CCOLS), BF16),
        dma((5,)),
        dma((4, N_ROW)),
        dma((4, N_ROW)),
        dma((2,)),
        dma((2,)),
        dma((2, 11)),
        dma((2, 11)),
        dma((FRAMES, 19)),
        dma((FRAMES, 19)),
        dma((STEPS, 9)),
        dma((STEPS, 9)),
    ]
    result = pl.pallas_call(
        kernel,
        out_shape=jax.ShapeDtypeStruct((FRAMES, BLOCK, D), BF16),
        in_specs=[any_spec, vmem_spec, any_spec, vmem_spec] + [any_spec] * 4,
        out_specs=vmem_spec,
        scratch_shapes=scratch,
        compiler_params=pltpu.CompilerParams(
            collective_id=0, has_side_effects=True, vmem_limit_bytes=62 * 2**20
        ),
        cost_estimate=pl.CostEstimate(flops=14_000_000_000, bytes_accessed=6 * 2**20, transcendentals=2**20),
    )(
        stream.reshape(FRAMES, BLOCK, D),
        mixer_gain,
        spectrum.reshape(2, BLOCK, D),
        mlp_gain,
        gate_weight[0],
        up_weight[0],
        down_weight[0],
        tables(),
    )
    return result.reshape(stream.shape)


def solution(mesh):
    return jax.shard_map(
        body,
        mesh=mesh,
        in_specs=(
            P("segment", "frame", "row", None, None),
            P("segment", None),
            P("segment", None, "row", None, None),
            P("segment", None),
            P("segment", "frame", "row"),
            P("segment", "frame", "row"),
            P("segment", "frame", "row"),
        ),
        out_specs=P("segment", "frame", "row", None, None),
        check_vma=False,
    )
```

```python
import functools
import math

import jax
import jax.numpy as jnp
import numpy as np
from jax import lax
from jax.experimental import pallas as pl
from jax.experimental.pallas import tpu as pltpu
from jax.sharding import PartitionSpec as P

MESH = pl.DeviceIdType.MESH
BF16, F32 = jnp.bfloat16, jnp.float32

N_ROW, N_Y, N_Z = 16, 4, 8
FRAMES = 2
BLOCK = 64
TOKENS = N_ROW * BLOCK
LANES = 128
D, HID, WROWS = 2048, 512, 256
OWN = 3
STEPS = FRAMES * N_Z
CCOLS = D // N_Z
LAGS = (1, 4, 7, 10)
LIVE = LAGS[-1] + 1


def tables():
    n = 32
    index = np.arange(n)
    angle = (index[:, None] * index[None, :] % n) * (2.0 * math.pi / n)
    cos, sin = np.cos(angle), np.sin(angle)
    cos[np.abs(cos) < 1e-9] = 0.0
    sin[np.abs(sin) < 1e-9] = 0.0
    eye4, eye8 = np.eye(4), np.eye(8)
    fwd = np.stack((cos, -sin))
    col = np.einsum("cwk,hg->kchgw", fwd, eye8).reshape(512, 256)
    mix = np.empty((2, 2, n, n))
    mix[0, 0], mix[0, 1], mix[1, 0], mix[1, 1] = cos, -sin, sin, cos
    row = np.einsum("cejhm,kl->ekmjlch", mix.reshape(2, 2, 4, 8, n), eye4).reshape(256, 256)
    inv = np.empty((2, 2, n, n))
    inv[0, 0], inv[0, 1], inv[1, 0], inv[1, 1] = cos, sin, -sin, cos
    irow = np.einsum("cemah,kl->ahkeclm", inv.reshape(2, 2, n, 8, 4), eye4).reshape(256, 256)
    icol = np.einsum("eakw,hg->hwagke", fwd.reshape(2, 8, 4, n), eye4).reshape(128, 256)
    return jnp.asarray(np.concatenate((col, row, irow, icol)), BF16)


def kernel(
    stream, mixer_gain_ref, spectrum, mlp_gain_ref, gate_w, up_w, down_w,
    tables_ref,
    out_ref,
    out, table, mixer_gain, mlp_gain, own_stream, rx_stream, rx_spec, aux_tx, aux_rx, rs_full, normed, col_buf, spec_buf, back_buf,
    full, wgu, wd, gain_col, folded, scales, acc, hid,
    part, sib_tx, sib_rx,
    x1_tx, x1_rx, y2_tx, y2_rx, y3_tx, y3_rx, x4_tx, x4_rx, y5_tx, y5_rx,
    loc, outs, a2a_s, a2a_r, spec_s, spec_r, zs, zr, ags, agr, rss, rsr,
):
    seg, z, me = lax.axis_index("segment"), lax.axis_index("frame"), lax.axis_index("row")
    core, xh, y = me % 2, (me // 2) % 2, me // 4
    row_of = lambda yy, xx, cc: (yy * 2 + xx) * 2 + cc
    ym, yp, y2 = (y + 3) % 4, (y + 1) % 4, (y + 2) % 4
    zm, zp = (z + 7) % 8, (z + 1) % 8
    to_yp, to_ym = (seg, z, row_of(yp, xh, core)), (seg, z, row_of(ym, xh, core))
    to_x, to_sib = (seg, z, row_of(y, 1 - xh, core)), (seg, z, row_of(y, xh, 1 - core))
    to_zp, to_zm = (seg, zp, me), (seg, zm, me)

    def remote(src, dst, ssem, rsem, to):
        return pltpu.make_async_remote_copy(
            src_ref=src, dst_ref=dst, send_sem=ssem, recv_sem=rsem, device_id=to, device_id_type=MESH
        )

    load_stream = pltpu.make_async_copy(stream, own_stream, loc.at[0])
    load_stream.start()
    load_table = pltpu.make_async_copy(tables_ref, table, loc.at[4])
    load_table.start()
    load_gains = [
        pltpu.make_async_copy(mixer_gain_ref, mixer_gain, loc.at[5]),
        pltpu.make_async_copy(mlp_gain_ref, mlp_gain, loc.at[6]),
    ]
    for copy in load_gains:
        copy.start()
    own_w = [
        pltpu.make_async_copy(gate_w, wgu.at[0, OWN], loc.at[1]),
        pltpu.make_async_copy(up_w, wgu.at[1, OWN], loc.at[2]),
        pltpu.make_async_copy(down_w, wd.at[OWN], loc.at[3]),
    ]
    for copy in own_w:
        copy.start()

    t_col, t_row, t_irow, t_icol = (table.at[a:b] for a, b in ((0, 512), (512, 768), (768, 1024), (1024, 1152)))

    barrier = pltpu.get_barrier_semaphore()

    def greet(j, _):
        pl.semaphore_signal(barrier, inc=1, device_id=(1 - seg, z, j), device_id_type=MESH)
        return 0

    lax.fori_loop(0, N_ROW, greet, 0)
    for to in (to_yp, to_ym, to_x, to_sib, to_zp, to_zm):
        pl.semaphore_signal(barrier, inc=1, device_id=to, device_id_type=MESH)
    pl.semaphore_wait(barrier, N_ROW + 6)

    def landing(kind, j):
        if kind < 2:
            return rx_stream.at[j, kind]
        return aux_rx.at[j] if kind == 2 else rx_spec.at[j, z % 2]

    def slab(kind, j):
        cols = pl.ds(pl.multiple_of(j * LANES, LANES), LANES)
        if kind < 2:
            src = stream.at[kind, :, cols]
        else:
            src = aux_tx.at[j] if kind == 2 else spectrum.at[z % 2, :, cols]
        return remote(src, landing(kind, me), a2a_s.at[kind, j], a2a_r.at[kind, me], (1 - seg, z, j))

    def send_slabs(kind):
        def step(j, _):
            slab(kind, (me + j) % N_ROW).start()
            return 0

        lax.fori_loop(0, N_ROW, step, 0)

    def wait_slabs(kind):
        def step(j, _):
            ref = landing(kind, j)
            remote(ref, ref, a2a_s.at[kind, j], a2a_r.at[kind, j], (1 - seg, z, j)).wait_recv()
            return 0

        lax.fori_loop(0, N_ROW, step, 0)

    def other_part(m, recv=False):
        to, slots = ((to_zp, pl.ds(0, N_ROW // 2)), (to_zm, pl.ds(N_ROW // 2, N_ROW // 2)))[m]
        ref = rx_spec.at[slots, (z + 1) % 2 if recv else z % 2]
        return remote(ref, ref, spec_s.at[m], spec_r.at[m], to)

    half = (pl.ds(0, WROWS // 2), pl.ds(WROWS // 2, WROWS // 2))

    def ring(step, way):
        k = step // 2 + 1 if step < 6 else 4 if step == 6 else step - 6
        sign = -1 if way == 0 else 1
        was, now = OWN + sign * (k - 1), (OWN + sign * k) % N_Z
        if step < 7:
            n = step % 2 if step < 6 else way
            dst = wgu.at[n, now]
            src = wgu.at[n, was] if step > 1 else (gate_w, up_w)[n]
        elif step < 10:
            dst = wd.at[now]
            src = wd.at[was] if step > 7 else down_w
        else:
            src, dst = wd.at[was, half[way]], wd.at[now, half[way]]
        return remote(src, dst, zs.at[way, step], zr.at[way, step], (to_zp, to_zm)[way])

    def ring_send(step, ways=(0, 1)):
        for way in ways:
            ring(step, way).start()

    def ring_wait(step):
        for way in (0, 1):
            ring(step, way).wait_recv()

    send_slabs(3)
    send_slabs(0)
    ring_send(0)

    load_stream.wait()
    for copy in load_gains:
        copy.wait()
    rows = FRAMES * BLOCK
    wide = own_stream[...].reshape(rows, D).astype(F32)
    mean_square = jnp.mean(wide * wide, axis=-1, keepdims=True)
    scale = lax.rsqrt(mean_square + 1e-05)
    across = jnp.broadcast_to(scale, (rows, rows)).T
    for j in range(N_ROW):
        aux_tx[j, 0:4, :] = across[0:4, :]
        aux_tx[j, 4:8, :] = jnp.broadcast_to(mixer_gain[:, j * LANES : (j + 1) * LANES], (4, LANES))
    send_slabs(2)
    send_slabs(1)
    wait_slabs(3)
    for m in range(2):
        other_part(m).start()
    ring_send(1)

    for j in range(N_ROW):
        gain_col[j] = jnp.broadcast_to(mlp_gain[:, j * LANES : (j + 1) * LANES], (LANES, LANES)).T
    ring_wait(0)
    ring_send(2)

    wait_slabs(0)
    wait_slabs(2)

    def spread(j, _):
        rs_full[j] = jnp.broadcast_to(aux_rx[j, 0:1, :], (rows, rows)).T
        return 0

    lax.fori_loop(0, N_ROW, spread, 0)

    def mixer_columns(f):
        def scale_step(j, _):
            values = rx_stream[j, f].astype(F32)
            factor = rs_full[j, f * BLOCK : (f + 1) * BLOCK, :]
            normed[f, j] = (values * factor * aux_rx[j, 4:5, :]).astype(BF16)
            return 0

        lax.fori_loop(0, N_ROW, scale_step, 0)
        for j in range(4):
            block = normed[f, 4 * j : 4 * j + 4].reshape(256, LANES)
            col_buf[f, j] = jnp.dot(t_col[...], block, preferred_element_type=F32).astype(BF16)

    def mixer_rows(f):
        for kg in range(8):
            pencils = jnp.concatenate([col_buf[f, j, kg * 64 : (kg + 1) * 64, :] for j in range(4)], axis=0)
            spec_buf[f, kg] = jnp.dot(t_row[...], pencils, preferred_element_type=F32)

    def mixer_filter(f):
        for kg in range(8):
            re, im = spec_buf[f, kg, :128], spec_buf[f, kg, 128:]
            f_re = jnp.concatenate([rx_spec[2 * kg, 0], rx_spec[2 * kg + 1, 0]], axis=0).astype(F32)
            f_im = jnp.concatenate([rx_spec[2 * kg, 1], rx_spec[2 * kg + 1, 1]], axis=0).astype(F32)
            filtered = jnp.concatenate([re * f_re - im * f_im, re * f_im + im * f_re], axis=0)
            back = jnp.dot(t_irow[...], filtered.astype(BF16), preferred_element_type=F32)
            back_buf[kg] = back.astype(BF16)
        for hb in range(8):
            pencils = jnp.concatenate([back_buf[kg, hb * 32 : (hb + 1) * 32, :] for kg in range(8)], axis=0)
            conv = jnp.dot(t_icol[...], pencils, preferred_element_type=F32) * (1.0 / 1024.0)
            values = rx_stream[2 * hb : 2 * hb + 2, f].reshape(128, LANES).astype(F32)
            scaled = normed[f, 2 * hb : 2 * hb + 2].reshape(128, LANES).astype(F32)
            mixed = (values + scaled * conv).astype(BF16)
            full[me, f, hb * BLOCK : (hb + 1) * BLOCK, :] = mixed[:BLOCK]
            full[me, f, 512 + hb * BLOCK : 512 + (hb + 1) * BLOCK, :] = mixed[BLOCK:]

    r = lambda yy, xx: row_of(yy, xx, core)
    xo = 1 - xh
    planes = (pl.ds(0, 512), pl.ds(512, 512))
    routes = [
        (me, None, to_yp, r(ym, xh)),
        (me, None, to_ym, r(yp, xh)),
        (me, None, to_x, r(y, xo)),
        (r(ym, xh), 0, to_yp, r(y2, xh)),
        (r(yp, xh), 1, to_ym, r(y2, xh)),
        (r(y, xo), None, to_yp, r(ym, xo)),
        (r(y, xo), None, to_ym, r(yp, xo)),
        (r(y2, xh), 0, to_x, r(y2, xo)),
        (r(y2, xh), 1, to_x, r(y2, xo)),
    ]
    handed = [
        (me, None), (r(ym, xh), None), (r(yp, xh), None), (r(y, xo), None), (r(y2, xh), 0), (r(y2, xh), 1),
        (r(ym, xo), None), (r(yp, xo), None), (r(y2, xo), 0), (r(y2, xo), 1),
    ]
    flip = lambda slot: slot + 1 - 2 * core
    for slot, plane in handed:
        routes.append((slot, plane, to_sib, flip(slot)))

    def gather(f, m, recv=False):
        sent, plane, to, got = routes[m]
        slot = got if recv else sent
        ref = full.at[slot, f] if plane is None else full.at[slot, f, planes[plane]]
        return remote(ref, ref, ags.at[f, m], agr.at[f, m], to)

    def g_send(f, *ms):
        for m in ms:
            gather(f, m).start()

    def g_wait(f, *ms):
        for m in ms:
            gather(f, m, True).wait_recv()

    def fold(slot, *kinds):
        zz = (z + slot + N_Z - OWN) % N_Z
        for n in kinds:
            for m in range(2):
                gain = gain_col[2 * zz + m]
                for c in range(0, HID, LANES):
                    at = (n, slot, slice(m * LANES, (m + 1) * LANES), slice(c, c + LANES))
                    folded[at] = (wgu[at].astype(F32) * gain).astype(BF16)

    most = (N_Z - 1) * WROWS

    def mlp_most(f, t):
        span = pl.ds(pl.multiple_of(t * 256, 256), 256)
        total = jnp.zeros((256, LANES), F32)
        for j in range(N_ROW):
            v = full[j, f, span, :].astype(F32)
            total = total + v * v
        scale = lax.rsqrt(jnp.sum(total, axis=-1, keepdims=True) * (1.0 / D) + 1e-05)
        scales[f, span, :] = jnp.broadcast_to(scale, (256, LANES))
        zs_of = [(z + slot + N_Z - OWN) % N_Z for slot in range(N_Z - 1)]
        values = jnp.concatenate([full[2 * zz + n, f, span, :] for zz in zs_of for n in range(2)], axis=1)
        for n in range(2):
            weight = folded[n, : N_Z - 1].reshape(most, HID)
            acc[n, f, span, :] = jnp.dot(values, weight, preferred_element_type=F32)

    def mlp_rest(f, t):
        span = pl.ds(pl.multiple_of(t * 256, 256), 256)
        zz = (z + N_Z - 1 - OWN) % N_Z
        last = jnp.concatenate([full[2 * zz, f, span, :], full[2 * zz + 1, f, span, :]], axis=1)
        scale = scales[f, span, 0:1]
        gate = (acc[0, f, span, :] + jnp.dot(last, folded[0, N_Z - 1], preferred_element_type=F32)) * scale
        up = (acc[1, f, span, :] + jnp.dot(last, folded[1, N_Z - 1], preferred_element_type=F32)) * scale
        hid[f, span, :] = (gate / (1.0 + jnp.exp(-gate)) * up).astype(BF16)

    load_table.wait()
    mixer_columns(0)
    mixer_rows(0)
    for m in range(2):
        other_part(m, True).wait_recv()
    for copy in own_w:
        copy.wait()
    mixer_filter(0)
    g_send(0, 0, 1, 2, 9)
    ring_wait(1)
    ring_send(3)
    wait_slabs(1)
    mixer_columns(1)
    mixer_rows(1)
    mixer_filter(1)
    g_send(1, 0, 1, 2, 9)
    fold(OWN, 0, 1)
    fold(OWN - 1, 0, 1)
    fold(OWN + 1, 0, 1)
    ring_wait(2)
    ring_send(4)
    g_wait(0, 0, 1)
    g_send(0, 3, 4, 10, 11)
    g_wait(1, 0, 1)
    g_send(1, 3, 4, 10, 11)
    g_wait(0, 2)
    g_send(0, 5, 6, 12)
    g_wait(1, 2)
    g_send(1, 5, 6, 12)
    ring_wait(3)
    ring_send(5)
    g_wait(0, 3, 4)
    g_send(0, 7, 8, 13, 14)
    fold(OWN - 2, 0, 1)
    fold(OWN + 2, 0, 1)
    g_wait(1, 3, 4)
    g_send(1, 7, 8, 13, 14)
    ring_wait(4)
    ring_send(6, (0,))
    g_wait(0, 5, 6)
    g_send(0, 15, 16)
    ring_wait(5)
    ring_send(6, (1,))
    ring_send(7)
    g_wait(0, 7, 8)
    g_send(0, 17, 18)
    fold(OWN - 3, 0, 1)
    fold(OWN + 3, 0, 1)
    g_wait(0, *range(9, 19))

    def tiles(part_of, f, lo, hi):
        def step(t, _):
            part_of(f, t)
            return 0

        lax.fori_loop(lo, hi, step, 0)

    tiles(mlp_most, 0, 0, 2)
    g_wait(1, 5, 6)
    g_send(1, 15, 16)
    tiles(mlp_most, 0, 2, 4)
    g_wait(1, 7, 8)
    g_send(1, 17, 18)
    g_wait(1, *range(9, 19))
    tiles(mlp_most, 1, 0, 4)
    ring_wait(6)
    ring_wait(7)
    ring_send(8)
    fold(N_Z - 1, 0, 1)
    tiles(mlp_rest, 0, 0, 4)

    q_same = lambda dy: ((y + dy + 4) % 4) * 2 + xh
    q_diff = lambda dy: ((y + dy + 4) % 4) * 2 + xo
    blk = lambda q: pl.ds(pl.multiple_of(q * BLOCK, BLOCK), BLOCK)
    low, high = pl.ds(0, BLOCK // 2), pl.ds(BLOCK // 2, BLOCK // 2)

    def reduce_copy(g, m):
        bufs = [
            (sib_tx.at[g], sib_rx.at[g], to_sib),
            (x1_tx.at[g], x1_rx.at[g], to_x),
            (y2_tx.at[g, 0], y2_rx.at[g, 0], to_yp),
            (y2_tx.at[g, 1], y2_rx.at[g, 1], to_ym),
            (y3_tx.at[g, 0], y3_rx.at[g, 0], to_yp),
            (y3_tx.at[g, 1], y3_rx.at[g, 1], to_ym),
            (x4_tx.at[g], x4_rx.at[g], to_x),
            (y5_tx.at[g, 0], y5_rx.at[g, 0], to_yp),
            (y5_tx.at[g, 1], y5_rx.at[g, 1], to_ym),
        ]
        src, dst, to = bufs[m]
        return remote(src, dst, rss.at[g, m], rsr.at[g, m], to)

    def place(g):
        late = g - 6
        f = jnp.where(g < 6, g // 3, jnp.where(g < 14, late // 2 % 2, g - 14))
        n = jnp.where(g < 6, g % 3, jnp.where(g < 14, 3 + late // 4 * 2 + late % 2, 7))
        return f, (n + 1) // 2 * (n % 2 * 2 - 1)

    def stage0(g):
        f, off = place(g)
        weight = wd[OWN + off]
        dims = (((1,), (1,)), ((), ()))
        other = hid[f, pl.ds(pl.multiple_of((1 - core) * 512, 512), 512), :]
        sib_tx[g] = lax.dot_general(other, weight, dims, preferred_element_type=F32).astype(BF16)
        reduce_copy(g, 0).start()
        mine = hid[f, pl.ds(pl.multiple_of(core * 512, 512), 512), :]
        part[g % LIVE] = lax.dot_general(mine, weight, dims, preferred_element_type=F32)

    def stage1(g):
        reduce_copy(g, 0).wait_recv()
        take = lambda q: part[g % LIVE, blk(q), :] + sib_rx[g, blk(q), :].astype(F32)
        x1_tx[g] = take(q_diff(2)).astype(BF16)
        reduce_copy(g, 1).start()
        y2_tx[g, 0] = take(q_diff(1)).astype(BF16)
        reduce_copy(g, 2).start()
        y2_tx[g, 1] = take(q_diff(-1)).astype(BF16)
        reduce_copy(g, 3).start()
        for q in (q_same(0), q_same(1), q_same(2), q_same(3), q_diff(0)):
            part[g % LIVE, blk(q), :] = take(q)

    def stage2(g):
        reduce_copy(g, 1).wait_recv()
        total = part[g % LIVE, blk(q_same(2)), :] + x1_rx[g].astype(F32)
        y3_tx[g, 0] = total[: BLOCK // 2].astype(BF16)
        y3_tx[g, 1] = total[BLOCK // 2 :].astype(BF16)
        reduce_copy(g, 4).start()
        reduce_copy(g, 5).start()
        reduce_copy(g, 2).wait_recv()
        reduce_copy(g, 3).wait_recv()
        total = part[g % LIVE, blk(q_diff(0)), :] + y2_rx[g, 0].astype(F32) + y2_rx[g, 1].astype(F32)
        x4_tx[g] = total.astype(BF16)
        reduce_copy(g, 6).start()

    def stage3(g):
        reduce_copy(g, 4).wait_recv()
        total = part[g % LIVE, blk(q_same(1)), :]
        first = total[: BLOCK // 2] + y3_rx[g, 0].astype(F32)
        y5_tx[g, 0] = jnp.concatenate([first, total[BLOCK // 2 :]], axis=0).astype(BF16)
        reduce_copy(g, 7).start()
        reduce_copy(g, 5).wait_recv()
        total = part[g % LIVE, blk(q_same(3)), :]
        second = total[BLOCK // 2 :] + y3_rx[g, 1].astype(F32)
        y5_tx[g, 1] = jnp.concatenate([total[: BLOCK // 2], second], axis=0).astype(BF16)
        reduce_copy(g, 8).start()

    def out_copy(g):
        f, off = place(g)
        cols = pl.ds(pl.multiple_of((z + off + N_Z) % N_Z * WROWS, WROWS), WROWS)
        return pltpu.make_async_copy(out.at[f, :, cols], out_ref.at[f, :, cols], outs.at[g])

    def stage4(g):
        f, off = place(g)
        zz = (z + off + N_Z) % N_Z
        for m in (6, 7, 8):
            reduce_copy(g, m).wait_recv()
        total = part[g % LIVE, blk(q_same(0)), :] + x4_rx[g].astype(F32)
        total = total + y5_rx[g, 0].astype(F32) + y5_rx[g, 1].astype(F32)
        mine = pl.ds(pl.multiple_of(core * 512 + q_same(0) * BLOCK, BLOCK), BLOCK)
        got = jnp.concatenate([full[2 * zz, f, mine, :], full[2 * zz + 1, f, mine, :]], axis=1)
        cols = pl.ds(pl.multiple_of(zz * 256, 256), 256)
        out[f, :, cols] = (got.astype(F32) + total).astype(BF16)
        out_copy(g).start()

    def step(g, _):
        for n, when in enumerate((4, 9)):

            @pl.when(g == when)
            def _(n=n):
                ring_wait(8 + n)
                ring_send(9 + n)

        @pl.when(g == 14)
        def _():
            ring_wait(10)

        @pl.when(g < STEPS)
        def _():
            stage0(g)

        for lag, stage in zip(LAGS, (stage1, stage2, stage3, stage4)):

            @pl.when((g >= lag) & (g < STEPS + lag))
            def _(lag=lag, stage=stage):
                stage(g - lag)

        @pl.when(g == 0)
        def _():
            tiles(mlp_rest, 1, 0, 4)

        return 0

    lax.fori_loop(0, STEPS + LAGS[-1], step, 0)

    def drain_slabs(j, _):
        for kind in range(4):
            slab(kind, j).wait_send()
        return 0

    lax.fori_loop(0, N_ROW, drain_slabs, 0)
    for m in range(2):
        other_part(m).wait_send()
    for way in (0, 1):
        for n in range(11):
            ring(n, way).wait_send()
    for f in range(FRAMES):
        for m in range(19):
            gather(f, m).wait_send()

    def drain_reduce(g, _):
        for m in range(9):
            reduce_copy(g, m).wait_send()
        out_copy(g).wait()
        return 0

    lax.fori_loop(0, STEPS, drain_reduce, 0)


def body(stream, mixer_gain, spectrum, mlp_gain, gate_weight, up_weight, down_weight):
    any_spec = pl.BlockSpec(memory_space=pl.ANY)
    dma = pltpu.SemaphoreType.DMA
    scratch = [
        pltpu.VMEM((FRAMES, BLOCK, D), BF16),
        pltpu.VMEM((1152, 256), BF16),
        pltpu.VMEM((1, D), F32),
        pltpu.VMEM((1, D), F32),
        pltpu.VMEM((FRAMES, BLOCK, D), BF16),
        pltpu.VMEM((N_ROW, FRAMES, BLOCK, LANES), BF16),
        pltpu.VMEM((N_ROW, 2, BLOCK, LANES), BF16),
        pltpu.VMEM((N_ROW, 8, LANES), F32),
        pltpu.VMEM((N_ROW, 8, LANES), F32),
        pltpu.VMEM((N_ROW, LANES, LANES), F32),
        pltpu.VMEM((FRAMES, N_ROW, BLOCK, LANES), BF16),
        pltpu.VMEM((FRAMES, 4, 512, LANES), BF16),
        pltpu.VMEM((FRAMES, 8, 256, LANES), F32),
        pltpu.VMEM((8, 256, LANES), BF16),
        pltpu.VMEM((N_ROW, FRAMES, TOKENS, LANES), BF16),
        pltpu.VMEM((2, N_Z, WROWS, HID), BF16),
        pltpu.VMEM((N_Z, WROWS, HID), BF16),
        pltpu.VMEM((N_ROW, LANES, LANES), F32),
        pltpu.VMEM((2, N_Z, WROWS, HID), BF16),
        pltpu.VMEM((FRAMES, TOKENS, LANES), F32),
        pltpu.VMEM((2, FRAMES, TOKENS, HID), F32),
        pltpu.VMEM((FRAMES, TOKENS, HID), BF16),
        pltpu.VMEM((LIVE, 512, CCOLS), F32),
        pltpu.VMEM((STEPS, 512, CCOLS), BF16),
        pltpu.VMEM((STEPS, 512, CCOLS), BF16),
        pltpu.VMEM((STEPS, BLOCK, CCOLS), BF16),
        pltpu.VMEM((STEPS, BLOCK, CCOLS), BF16),
        pltpu.VMEM((STEPS, 2, BLOCK, CCOLS), BF16),
        pltpu.VMEM((STEPS, 2, BLOCK, CCOLS), BF16),
        pltpu.VMEM((STEPS, 2, BLOCK // 2, CCOLS), BF16),
        pltpu.VMEM((STEPS, 2, BLOCK // 2, CCOLS), BF16),
        pltpu.VMEM((STEPS, BLOCK, CCOLS), BF16),
        pltpu.VMEM((STEPS, BLOCK, CCOLS), BF16),
        pltpu.VMEM((STEPS, 2, BLOCK, CCOLS), BF16),
        pltpu.VMEM((STEPS, 2, BLOCK, CCOLS), BF16),
        dma((7,)),
        dma((STEPS,)),
        dma((4, N_ROW)),
        dma((4, N_ROW)),
        dma((2,)),
        dma((2,)),
        dma((2, 11)),
        dma((2, 11)),
        dma((FRAMES, 19)),
        dma((FRAMES, 19)),
        dma((STEPS, 9)),
        dma((STEPS, 9)),
    ]
    result = pl.pallas_call(
        kernel,
        out_shape=jax.ShapeDtypeStruct((FRAMES, BLOCK, D), BF16),
        in_specs=[any_spec] * 8,
        out_specs=any_spec,
        scratch_shapes=scratch,
        compiler_params=pltpu.CompilerParams(
            collective_id=0, has_side_effects=True, vmem_limit_bytes=62 * 2**20
        ),
        cost_estimate=pl.CostEstimate(flops=14_000_000_000, bytes_accessed=6 * 2**20, transcendentals=2**20),
    )(
        stream.reshape(FRAMES, BLOCK, D),
        mixer_gain,
        spectrum.reshape(2, BLOCK, D),
        mlp_gain,
        gate_weight[0],
        up_weight[0],
        down_weight[0],
        tables(),
    )
    return result.reshape(stream.shape)


def solution(mesh):
    return jax.shard_map(
        body,
        mesh=mesh,
        in_specs=(
            P("segment", "frame", "row", None, None),
            P("segment", None),
            P("segment", None, "row", None, None),
            P("segment", None),
            P("segment", "frame", "row"),
            P("segment", "frame", "row"),
            P("segment", "frame", "row"),
        ),
        out_specs=P("segment", "frame", "row", None, None),
        check_vma=False,
    )
```

```python
import functools
import math

import jax
import jax.numpy as jnp
import numpy as np
from jax import lax
from jax.experimental import pallas as pl
from jax.experimental.pallas import tpu as pltpu
from jax.sharding import PartitionSpec as P

MESH = pl.DeviceIdType.MESH
BF16, F32 = jnp.bfloat16, jnp.float32

N_ROW, N_Y, N_Z = 16, 4, 8
FRAMES = 2
BLOCK = 64
TOKENS = N_ROW * BLOCK
LANES = 128
D, HID, WROWS = 2048, 512, 256
OWN = 3
STEPS = FRAMES * N_Z
CCOLS = D // N_Z
LAGS = (1, 4, 7, 10)
LIVE = LAGS[-1] + 1


def tables():
    n = 32
    index = np.arange(n)
    angle = (index[:, None] * index[None, :] % n) * (2.0 * math.pi / n)
    cos, sin = np.cos(angle), np.sin(angle)
    cos[np.abs(cos) < 1e-9] = 0.0
    sin[np.abs(sin) < 1e-9] = 0.0
    eye4, eye8 = np.eye(4), np.eye(8)
    fwd = np.stack((cos, -sin))
    col = np.einsum("cwk,hg->kchgw", fwd, eye8).reshape(512, 256)
    mix = np.empty((2, 2, n, n))
    mix[0, 0], mix[0, 1], mix[1, 0], mix[1, 1] = cos, -sin, sin, cos
    row = np.einsum("cejhm,kl->ekmjlch", mix.reshape(2, 2, 4, 8, n), eye4).reshape(256, 256)
    inv = np.empty((2, 2, n, n))
    inv[0, 0], inv[0, 1], inv[1, 0], inv[1, 1] = cos, sin, -sin, cos
    irow = np.einsum("cemah,kl->ahkeclm", inv.reshape(2, 2, n, 8, 4), eye4).reshape(256, 256)
    icol = np.einsum("eakw,hg->hwagke", fwd.reshape(2, 8, 4, n), eye4).reshape(128, 256)
    return jnp.asarray(np.concatenate((col, row, irow, icol)), BF16)


def kernel(
    stream, mixer_gain_ref, spectrum, mlp_gain_ref, gate_w, up_w, down_w,
    tables_ref,
    out_ref,
    out, table, mixer_gain, mlp_gain, own_stream, rx_stream, rx_spec, aux_tx, aux_rx, rs_full, normed, col_buf, spec_buf, back_buf,
    full, wgu, wd, gain_col, folded, scales, acc, hid,
    part, sib_tx, sib_rx,
    x1_tx, x1_rx, y2_tx, y2_rx, y3_tx, y3_rx, x4_tx, x4_rx, y5_tx, y5_rx,
    loc, outs, a2a_s, a2a_r, spec_s, spec_r, zs, zr, ags, agr, rss, rsr,
):
    seg, z, me = lax.axis_index("segment"), lax.axis_index("frame"), lax.axis_index("row")
    core, xh, y = me % 2, (me // 2) % 2, me // 4
    row_of = lambda yy, xx, cc: (yy * 2 + xx) * 2 + cc
    ym, yp, y2 = (y + 3) % 4, (y + 1) % 4, (y + 2) % 4
    zm, zp = (z + 7) % 8, (z + 1) % 8
    to_yp, to_ym = (seg, z, row_of(yp, xh, core)), (seg, z, row_of(ym, xh, core))
    to_x, to_sib = (seg, z, row_of(y, 1 - xh, core)), (seg, z, row_of(y, xh, 1 - core))
    to_zp, to_zm = (seg, zp, me), (seg, zm, me)

    def remote(src, dst, ssem, rsem, to):
        return pltpu.make_async_remote_copy(
            src_ref=src, dst_ref=dst, send_sem=ssem, recv_sem=rsem, device_id=to, device_id_type=MESH
        )

    load_stream = pltpu.make_async_copy(stream, own_stream, loc.at[0])
    load_stream.start()
    load_table = pltpu.make_async_copy(tables_ref, table, loc.at[4])
    load_table.start()
    load_gains = [
        pltpu.make_async_copy(mixer_gain_ref, mixer_gain, loc.at[5]),
        pltpu.make_async_copy(mlp_gain_ref, mlp_gain, loc.at[6]),
    ]
    for copy in load_gains:
        copy.start()
    own_w = [
        pltpu.make_async_copy(gate_w, wgu.at[0, OWN], loc.at[1]),
        pltpu.make_async_copy(up_w, wgu.at[1, OWN], loc.at[2]),
        pltpu.make_async_copy(down_w, wd.at[OWN], loc.at[3]),
    ]
    for copy in own_w:
        copy.start()

    t_col, t_row, t_irow, t_icol = (table.at[a:b] for a, b in ((0, 512), (512, 768), (768, 1024), (1024, 1152)))

    barrier = pltpu.get_barrier_semaphore()

    def greet(j, _):
        pl.semaphore_signal(barrier, inc=1, device_id=(1 - seg, z, j), device_id_type=MESH)
        return 0

    lax.fori_loop(0, N_ROW, greet, 0, unroll=True)
    for to in (to_yp, to_ym, to_x, to_sib, to_zp, to_zm):
        pl.semaphore_signal(barrier, inc=1, device_id=to, device_id_type=MESH)
    pl.semaphore_wait(barrier, N_ROW + 6)

    def landing(kind, j):
        if kind < 2:
            return rx_stream.at[j, kind]
        return aux_rx.at[j] if kind == 2 else rx_spec.at[j, z % 2]

    def slab(kind, j):
        cols = pl.ds(pl.multiple_of(j * LANES, LANES), LANES)
        if kind < 2:
            src = stream.at[kind, :, cols]
        else:
            src = aux_tx.at[j] if kind == 2 else spectrum.at[z % 2, :, cols]
        return remote(src, landing(kind, me), a2a_s.at[kind, j], a2a_r.at[kind, me], (1 - seg, z, j))

    def send_slabs(kind):
        def step(j, _):
            slab(kind, (me + j) % N_ROW).start()
            return 0

        lax.fori_loop(0, N_ROW, step, 0, unroll=True)

    def wait_slabs(kind):
        def step(j, _):
            ref = landing(kind, j)
            remote(ref, ref, a2a_s.at[kind, j], a2a_r.at[kind, j], (1 - seg, z, j)).wait_recv()
            return 0

        lax.fori_loop(0, N_ROW, step, 0, unroll=True)

    def other_part(m, recv=False):
        to, slots = ((to_zp, pl.ds(0, N_ROW // 2)), (to_zm, pl.ds(N_ROW // 2, N_ROW // 2)))[m]
        ref = rx_spec.at[slots, (z + 1) % 2 if recv else z % 2]
        return remote(ref, ref, spec_s.at[m], spec_r.at[m], to)

    half = (pl.ds(0, WROWS // 2), pl.ds(WROWS // 2, WROWS // 2))

    def ring(step, way):
        k = step // 2 + 1 if step < 6 else 4 if step == 6 else step - 6
        sign = -1 if way == 0 else 1
        was, now = OWN + sign * (k - 1), (OWN + sign * k) % N_Z
        if step < 7:
            n = step % 2 if step < 6 else way
            dst = wgu.at[n, now]
            src = wgu.at[n, was] if step > 1 else (gate_w, up_w)[n]
        elif step < 10:
            dst = wd.at[now]
            src = wd.at[was] if step > 7 else down_w
        else:
            src, dst = wd.at[was, half[way]], wd.at[now, half[way]]
        return remote(src, dst, zs.at[way, step], zr.at[way, step], (to_zp, to_zm)[way])

    def ring_send(step, ways=(0, 1)):
        for way in ways:
            ring(step, way).start()

    def ring_wait(step):
        for way in (0, 1):
            ring(step, way).wait_recv()

    send_slabs(3)
    send_slabs(0)
    ring_send(0)

    load_stream.wait()
    for copy in load_gains:
        copy.wait()
    rows = FRAMES * BLOCK
    wide = own_stream[...].reshape(rows, D).astype(F32)
    mean_square = jnp.mean(wide * wide, axis=-1, keepdims=True)
    scale = lax.rsqrt(mean_square + 1e-05)
    across = jnp.broadcast_to(scale, (rows, rows)).T
    for j in range(N_ROW):
        aux_tx[j, 0:4, :] = across[0:4, :]
        aux_tx[j, 4:8, :] = jnp.broadcast_to(mixer_gain[:, j * LANES : (j + 1) * LANES], (4, LANES))
    send_slabs(2)
    send_slabs(1)
    wait_slabs(3)
    for m in range(2):
        other_part(m).start()
    ring_send(1)

    for j in range(N_ROW):
        gain_col[j] = jnp.broadcast_to(mlp_gain[:, j * LANES : (j + 1) * LANES], (LANES, LANES)).T
    ring_wait(0)
    ring_send(2)

    wait_slabs(0)
    wait_slabs(2)

    def spread(j, _):
        rs_full[j] = jnp.broadcast_to(aux_rx[j, 0:1, :], (rows, rows)).T
        return 0

    lax.fori_loop(0, N_ROW, spread, 0)

    def mixer_columns(f):
        def scale_step(j, _):
            values = rx_stream[j, f].astype(F32)
            factor = rs_full[j, f * BLOCK : (f + 1) * BLOCK, :]
            normed[f, j] = (values * factor * aux_rx[j, 4:5, :]).astype(BF16)
            return 0

        lax.fori_loop(0, N_ROW, scale_step, 0)
        for j in range(4):
            block = normed[f, 4 * j : 4 * j + 4].reshape(256, LANES)
            col_buf[f, j] = jnp.dot(t_col[...], block, preferred_element_type=F32).astype(BF16)

    def mixer_rows(f):
        for kg in range(8):
            pencils = jnp.concatenate([col_buf[f, j, kg * 64 : (kg + 1) * 64, :] for j in range(4)], axis=0)
            spec_buf[f, kg] = jnp.dot(t_row[...], pencils, preferred_element_type=F32)

    def mixer_filter(f):
        for kg in range(8):
            re, im = spec_buf[f, kg, :128], spec_buf[f, kg, 128:]
            f_re = jnp.concatenate([rx_spec[2 * kg, 0], rx_spec[2 * kg + 1, 0]], axis=0).astype(F32)
            f_im = jnp.concatenate([rx_spec[2 * kg, 1], rx_spec[2 * kg + 1, 1]], axis=0).astype(F32)
            filtered = jnp.concatenate([re * f_re - im * f_im, re * f_im + im * f_re], axis=0)
            back = jnp.dot(t_irow[...], filtered.astype(BF16), preferred_element_type=F32)
            back_buf[kg] = back.astype(BF16)
        for hb in range(8):
            pencils = jnp.concatenate([back_buf[kg, hb * 32 : (hb + 1) * 32, :] for kg in range(8)], axis=0)
            conv = jnp.dot(t_icol[...], pencils, preferred_element_type=F32) * (1.0 / 1024.0)
            values = rx_stream[2 * hb : 2 * hb + 2, f].reshape(128, LANES).astype(F32)
            scaled = normed[f, 2 * hb : 2 * hb + 2].reshape(128, LANES).astype(F32)
            mixed = (values + scaled * conv).astype(BF16)
            full[me, f, hb * BLOCK : (hb + 1) * BLOCK, :] = mixed[:BLOCK]
            full[me, f, 512 + hb * BLOCK : 512 + (hb + 1) * BLOCK, :] = mixed[BLOCK:]

    r = lambda yy, xx: row_of(yy, xx, core)
    xo = 1 - xh
    planes = (pl.ds(0, 512), pl.ds(512, 512))
    routes = [
        (me, None, to_yp, r(ym, xh)),
        (me, None, to_ym, r(yp, xh)),
        (me, None, to_x, r(y, xo)),
        (r(ym, xh), 0, to_yp, r(y2, xh)),
        (r(yp, xh), 1, to_ym, r(y2, xh)),
        (r(y, xo), None, to_yp, r(ym, xo)),
        (r(y, xo), None, to_ym, r(yp, xo)),
        (r(y2, xh), 0, to_x, r(y2, xo)),
        (r(y2, xh), 1, to_x, r(y2, xo)),
    ]
    handed = [
        (me, None), (r(ym, xh), None), (r(yp, xh), None), (r(y, xo), None), (r(y2, xh), 0), (r(y2, xh), 1),
        (r(ym, xo), None), (r(yp, xo), None), (r(y2, xo), 0), (r(y2, xo), 1),
    ]
    flip = lambda slot: slot + 1 - 2 * core
    for slot, plane in handed:
        routes.append((slot, plane, to_sib, flip(slot)))

    def gather(f, m, recv=False):
        sent, plane, to, got = routes[m]
        slot = got if recv else sent
        ref = full.at[slot, f] if plane is None else full.at[slot, f, planes[plane]]
        return remote(ref, ref, ags.at[f, m], agr.at[f, m], to)

    def g_send(f, *ms):
        for m in ms:
            gather(f, m).start()

    def g_wait(f, *ms):
        for m in ms:
            gather(f, m, True).wait_recv()

    def fold(slot, *kinds):
        zz = (z + slot + N_Z - OWN) % N_Z
        for n in kinds:
            for m in range(2):
                gain = gain_col[2 * zz + m]
                for c in range(0, HID, LANES):
                    at = (n, slot, slice(m * LANES, (m + 1) * LANES), slice(c, c + LANES))
                    folded[at] = (wgu[at].astype(F32) * gain).astype(BF16)

    most = (N_Z - 1) * WROWS

    def mlp_most(f, t):
        span = pl.ds(pl.multiple_of(t * 256, 256), 256)
        total = jnp.zeros((256, LANES), F32)
        for j in range(N_ROW):
            v = full[j, f, span, :].astype(F32)
            total = total + v * v
        scale = lax.rsqrt(jnp.sum(total, axis=-1, keepdims=True) * (1.0 / D) + 1e-05)
        scales[f, span, :] = jnp.broadcast_to(scale, (256, LANES))
        zs_of = [(z + slot + N_Z - OWN) % N_Z for slot in range(N_Z - 1)]
        values = jnp.concatenate([full[2 * zz + n, f, span, :] for zz in zs_of for n in range(2)], axis=1)
        for n in range(2):
            weight = folded[n, : N_Z - 1].reshape(most, HID)
            acc[n, f, span, :] = jnp.dot(values, weight, preferred_element_type=F32)

    def mlp_rest(f, t):
        span = pl.ds(pl.multiple_of(t * 256, 256), 256)
        zz = (z + N_Z - 1 - OWN) % N_Z
        last = jnp.concatenate([full[2 * zz, f, span, :], full[2 * zz + 1, f, span, :]], axis=1)
        scale = scales[f, span, 0:1]
        gate = (acc[0, f, span, :] + jnp.dot(last, folded[0, N_Z - 1], preferred_element_type=F32)) * scale
        up = (acc[1, f, span, :] + jnp.dot(last, folded[1, N_Z - 1], preferred_element_type=F32)) * scale
        hid[f, span, :] = (gate / (1.0 + jnp.exp(-gate)) * up).astype(BF16)

    load_table.wait()
    mixer_columns(0)
    mixer_rows(0)
    for m in range(2):
        other_part(m, True).wait_recv()
    for copy in own_w:
        copy.wait()
    mixer_filter(0)
    g_send(0, 0, 1, 2, 9)
    ring_wait(1)
    ring_send(3)
    wait_slabs(1)
    mixer_columns(1)
    mixer_rows(1)
    mixer_filter(1)
    g_send(1, 0, 1, 2, 9)
    fold(OWN, 0, 1)
    fold(OWN - 1, 0, 1)
    fold(OWN + 1, 0, 1)
    ring_wait(2)
    ring_send(4)
    g_wait(0, 0, 1)
    g_send(0, 3, 4, 10, 11)
    g_wait(1, 0, 1)
    g_send(1, 3, 4, 10, 11)
    g_wait(0, 2)
    g_send(0, 5, 6, 12)
    g_wait(1, 2)
    g_send(1, 5, 6, 12)
    ring_wait(3)
    ring_send(5)
    g_wait(0, 3, 4)
    g_send(0, 7, 8, 13, 14)
    fold(OWN - 2, 0, 1)
    fold(OWN + 2, 0, 1)
    g_wait(1, 3, 4)
    g_send(1, 7, 8, 13, 14)
    ring_wait(4)
    ring_send(6, (0,))
    g_wait(0, 5, 6)
    g_send(0, 15, 16)
    ring_wait(5)
    ring_send(6, (1,))
    ring_send(7)
    g_wait(0, 7, 8)
    g_send(0, 17, 18)
    fold(OWN - 3, 0, 1)
    fold(OWN + 3, 0, 1)
    g_wait(0, *range(9, 19))

    def tiles(part_of, f, lo, hi):
        def step(t, _):
            part_of(f, t)
            return 0

        lax.fori_loop(lo, hi, step, 0)

    tiles(mlp_most, 0, 0, 2)
    g_wait(1, 5, 6)
    g_send(1, 15, 16)
    tiles(mlp_most, 0, 2, 4)
    g_wait(1, 7, 8)
    g_send(1, 17, 18)
    g_wait(1, *range(9, 19))
    tiles(mlp_most, 1, 0, 4)
    ring_wait(6)
    ring_wait(7)
    ring_send(8)
    fold(N_Z - 1, 0, 1)
    tiles(mlp_rest, 0, 0, 4)

    q_same = lambda dy: ((y + dy + 4) % 4) * 2 + xh
    q_diff = lambda dy: ((y + dy + 4) % 4) * 2 + xo
    blk = lambda q: pl.ds(pl.multiple_of(q * BLOCK, BLOCK), BLOCK)
    low, high = pl.ds(0, BLOCK // 2), pl.ds(BLOCK // 2, BLOCK // 2)

    def reduce_copy(g, m):
        bufs = [
            (sib_tx.at[g], sib_rx.at[g], to_sib),
            (x1_tx.at[g], x1_rx.at[g], to_x),
            (y2_tx.at[g, 0], y2_rx.at[g, 0], to_yp),
            (y2_tx.at[g, 1], y2_rx.at[g, 1], to_ym),
            (y3_tx.at[g, 0], y3_rx.at[g, 0], to_yp),
            (y3_tx.at[g, 1], y3_rx.at[g, 1], to_ym),
            (x4_tx.at[g], x4_rx.at[g], to_x),
            (y5_tx.at[g, 0], y5_rx.at[g, 0], to_yp),
            (y5_tx.at[g, 1], y5_rx.at[g, 1], to_ym),
        ]
        src, dst, to = bufs[m]
        return remote(src, dst, rss.at[g, m], rsr.at[g, m], to)

    def place(g):
        late = g - 6
        f = jnp.where(g < 6, g // 3, jnp.where(g < 14, late // 2 % 2, g - 14))
        n = jnp.where(g < 6, g % 3, jnp.where(g < 14, 3 + late // 4 * 2 + late % 2, 7))
        return f, (n + 1) // 2 * (n % 2 * 2 - 1)

    def stage0(g):
        f, off = place(g)
        weight = wd[OWN + off]
        dims = (((1,), (1,)), ((), ()))
        other = hid[f, pl.ds(pl.multiple_of((1 - core) * 512, 512), 512), :]
        sib_tx[g] = lax.dot_general(other, weight, dims, preferred_element_type=F32).astype(BF16)
        reduce_copy(g, 0).start()
        mine = hid[f, pl.ds(pl.multiple_of(core * 512, 512), 512), :]
        part[g % LIVE] = lax.dot_general(mine, weight, dims, preferred_element_type=F32)

    def stage1(g):
        reduce_copy(g, 0).wait_recv()
        take = lambda q: part[g % LIVE, blk(q), :] + sib_rx[g, blk(q), :].astype(F32)
        x1_tx[g] = take(q_diff(2)).astype(BF16)
        reduce_copy(g, 1).start()
        y2_tx[g, 0] = take(q_diff(1)).astype(BF16)
        reduce_copy(g, 2).start()
        y2_tx[g, 1] = take(q_diff(-1)).astype(BF16)
        reduce_copy(g, 3).start()
        for q in (q_same(0), q_same(1), q_same(2), q_same(3), q_diff(0)):
            part[g % LIVE, blk(q), :] = take(q)

    def stage2(g):
        reduce_copy(g, 1).wait_recv()
        total = part[g % LIVE, blk(q_same(2)), :] + x1_rx[g].astype(F32)
        y3_tx[g, 0] = total[: BLOCK // 2].astype(BF16)
        y3_tx[g, 1] = total[BLOCK // 2 :].astype(BF16)
        reduce_copy(g, 4).start()
        reduce_copy(g, 5).start()
        reduce_copy(g, 2).wait_recv()
        reduce_copy(g, 3).wait_recv()
        total = part[g % LIVE, blk(q_diff(0)), :] + y2_rx[g, 0].astype(F32) + y2_rx[g, 1].astype(F32)
        x4_tx[g] = total.astype(BF16)
        reduce_copy(g, 6).start()

    def stage3(g):
        reduce_copy(g, 4).wait_recv()
        total = part[g % LIVE, blk(q_same(1)), :]
        first = total[: BLOCK // 2] + y3_rx[g, 0].astype(F32)
        y5_tx[g, 0] = jnp.concatenate([first, total[BLOCK // 2 :]], axis=0).astype(BF16)
        reduce_copy(g, 7).start()
        reduce_copy(g, 5).wait_recv()
        total = part[g % LIVE, blk(q_same(3)), :]
        second = total[BLOCK // 2 :] + y3_rx[g, 1].astype(F32)
        y5_tx[g, 1] = jnp.concatenate([total[: BLOCK // 2], second], axis=0).astype(BF16)
        reduce_copy(g, 8).start()

    def out_copy(g):
        f, off = place(g)
        cols = pl.ds(pl.multiple_of((z + off + N_Z) % N_Z * WROWS, WROWS), WROWS)
        return pltpu.make_async_copy(out.at[f, :, cols], out_ref.at[f, :, cols], outs.at[g])

    def stage4(g):
        f, off = place(g)
        zz = (z + off + N_Z) % N_Z
        for m in (6, 7, 8):
            reduce_copy(g, m).wait_recv()
        total = part[g % LIVE, blk(q_same(0)), :] + x4_rx[g].astype(F32)
        total = total + y5_rx[g, 0].astype(F32) + y5_rx[g, 1].astype(F32)
        mine = pl.ds(pl.multiple_of(core * 512 + q_same(0) * BLOCK, BLOCK), BLOCK)
        got = jnp.concatenate([full[2 * zz, f, mine, :], full[2 * zz + 1, f, mine, :]], axis=1)
        cols = pl.ds(pl.multiple_of(zz * 256, 256), 256)
        out[f, :, cols] = (got.astype(F32) + total).astype(BF16)
        out_copy(g).start()

    def step(g, _):
        for n, when in enumerate((5, 10)):

            @pl.when(g == when)
            def _(n=n):
                ring_wait(8 + n)
                ring_send(9 + n)

        @pl.when(g == 14)
        def _():
            ring_wait(10)

        @pl.when(g < STEPS)
        def _():
            stage0(g)

        for lag, stage in zip(LAGS, (stage1, stage2, stage3, stage4)):

            @pl.when((g >= lag) & (g < STEPS + lag))
            def _(lag=lag, stage=stage):
                stage(g - lag)

        @pl.when(g == 0)
        def _():
            tiles(mlp_rest, 1, 0, 4)

        return 0

    lax.fori_loop(0, STEPS + LAGS[-1], step, 0)

    def drain_slabs(j, _):
        for kind in range(4):
            slab(kind, j).wait_send()
        return 0

    lax.fori_loop(0, N_ROW, drain_slabs, 0)
    for m in range(2):
        other_part(m).wait_send()
    for way in (0, 1):
        for n in range(11):
            ring(n, way).wait_send()
    for f in range(FRAMES):
        for m in range(19):
            gather(f, m).wait_send()

    def drain_reduce(g, _):
        for m in range(9):
            reduce_copy(g, m).wait_send()
        out_copy(g).wait()
        return 0

    lax.fori_loop(0, STEPS, drain_reduce, 0)


def body(stream, mixer_gain, spectrum, mlp_gain, gate_weight, up_weight, down_weight):
    any_spec = pl.BlockSpec(memory_space=pl.ANY)
    dma = pltpu.SemaphoreType.DMA
    scratch = [
        pltpu.VMEM((FRAMES, BLOCK, D), BF16),
        pltpu.VMEM((1152, 256), BF16),
        pltpu.VMEM((1, D), F32),
        pltpu.VMEM((1, D), F32),
        pltpu.VMEM((FRAMES, BLOCK, D), BF16),
        pltpu.VMEM((N_ROW, FRAMES, BLOCK, LANES), BF16),
        pltpu.VMEM((N_ROW, 2, BLOCK, LANES), BF16),
        pltpu.VMEM((N_ROW, 8, LANES), F32),
        pltpu.VMEM((N_ROW, 8, LANES), F32),
        pltpu.VMEM((N_ROW, LANES, LANES), F32),
        pltpu.VMEM((FRAMES, N_ROW, BLOCK, LANES), BF16),
        pltpu.VMEM((FRAMES, 4, 512, LANES), BF16),
        pltpu.VMEM((FRAMES, 8, 256, LANES), F32),
        pltpu.VMEM((8, 256, LANES), BF16),
        pltpu.VMEM((N_ROW, FRAMES, TOKENS, LANES), BF16),
        pltpu.VMEM((2, N_Z, WROWS, HID), BF16),
        pltpu.VMEM((N_Z, WROWS, HID), BF16),
        pltpu.VMEM((N_ROW, LANES, LANES), F32),
        pltpu.VMEM((2, N_Z, WROWS, HID), BF16),
        pltpu.VMEM((FRAMES, TOKENS, LANES), F32),
        pltpu.VMEM((2, FRAMES, TOKENS, HID), F32),
        pltpu.VMEM((FRAMES, TOKENS, HID), BF16),
        pltpu.VMEM((LIVE, 512, CCOLS), F32),
        pltpu.VMEM((STEPS, 512, CCOLS), BF16),
        pltpu.VMEM((STEPS, 512, CCOLS), BF16),
        pltpu.VMEM((STEPS, BLOCK, CCOLS), BF16),
        pltpu.VMEM((STEPS, BLOCK, CCOLS), BF16),
        pltpu.VMEM((STEPS, 2, BLOCK, CCOLS), BF16),
        pltpu.VMEM((STEPS, 2, BLOCK, CCOLS), BF16),
        pltpu.VMEM((STEPS, 2, BLOCK // 2, CCOLS), BF16),
        pltpu.VMEM((STEPS, 2, BLOCK // 2, CCOLS), BF16),
        pltpu.VMEM((STEPS, BLOCK, CCOLS), BF16),
        pltpu.VMEM((STEPS, BLOCK, CCOLS), BF16),
        pltpu.VMEM((STEPS, 2, BLOCK, CCOLS), BF16),
        pltpu.VMEM((STEPS, 2, BLOCK, CCOLS), BF16),
        dma((7,)),
        dma((STEPS,)),
        dma((4, N_ROW)),
        dma((4, N_ROW)),
        dma((2,)),
        dma((2,)),
        dma((2, 11)),
        dma((2, 11)),
        dma((FRAMES, 19)),
        dma((FRAMES, 19)),
        dma((STEPS, 9)),
        dma((STEPS, 9)),
    ]
    result = pl.pallas_call(
        kernel,
        out_shape=jax.ShapeDtypeStruct((FRAMES, BLOCK, D), BF16),
        in_specs=[any_spec] * 8,
        out_specs=any_spec,
        scratch_shapes=scratch,
        compiler_params=pltpu.CompilerParams(
            collective_id=0, has_side_effects=True, vmem_limit_bytes=62 * 2**20
        ),
        cost_estimate=pl.CostEstimate(flops=14_000_000_000, bytes_accessed=6 * 2**20, transcendentals=2**20),
    )(
        stream.reshape(FRAMES, BLOCK, D),
        mixer_gain,
        spectrum.reshape(2, BLOCK, D),
        mlp_gain,
        gate_weight[0],
        up_weight[0],
        down_weight[0],
        tables(),
    )
    return result.reshape(stream.shape)


def solution(mesh):
    return jax.shard_map(
        body,
        mesh=mesh,
        in_specs=(
            P("segment", "frame", "row", None, None),
            P("segment", None),
            P("segment", None, "row", None, None),
            P("segment", None),
            P("segment", "frame", "row"),
            P("segment", "frame", "row"),
            P("segment", "frame", "row"),
        ),
        out_specs=P("segment", "frame", "row", None, None),
        check_vma=False,
    )
```
